256 devices in a mesh: section: 4 (over y), shard: 32 (over x_lo, z, core), mp: 2 (over x_hi).
Axes of the slice: x: 4 (x_hi: 2, x_lo: 2; x = x_hi * 2 + x_lo), y: 4, z: 8, core: 2. Of those that a mesh axis runs over, the one named last changes fastest.
Arguments:
- queries: bfloat16 [32768, 1536], P(('section', 'shard'), 'mp'), may hold values from -6 to 6
- ctx_keys: bfloat16 [32768, 1536], P(('section', 'shard'), 'mp'), may hold values from -88 to 88
- ctx_values: bfloat16 [32768, 1536], P(('section', 'shard'), 'mp'), may hold values from -6 to 6
- cotangent: bfloat16 [32768, 1536], P(('section', 'shard'), 'mp'), may hold values from -6 to 6
- owner: int32 [512, 2], P(('section', 'shard')), may hold values from 0 to 31, all different within a row; in each aligned block of 4 rows (0 to 3, 4 to 7, ...) at most 2 rows name the same one
- slot_row: int32 [512, 2], P(('section', 'shard')), may hold values from 0 to 11
- database: bfloat16 [384, 64, 1536], P('shard'), may hold values from -6 to 6
- enc_gain: float32 [1536], replicated, may hold values from 0.25 to 1.75
- enc_query_w: bfloat16 [1536, 1536], P('section', 'mp'), may hold values from -0.15625 to 0.15625
- enc_out_w: bfloat16 [1536, 1536], P('section', 'mp'), may hold values from -0.15625 to 0.15625
Outputs:
- attended: bfloat16 [32768, 1536], P(('section', 'shard'), 'mp')
- grad_queries: bfloat16 [32768, 1536], P(('section', 'shard'), 'mp')
- grad_keys: bfloat16 [32768, 1536], P(('section', 'shard'), 'mp')
- grad_values: bfloat16 [32768, 1536], P(('section', 'shard'), 'mp')
The draws below stay inside these ranges and needn't reach their ends.
Inputs may be any that keep to these rules, and one draw needn't show every extreme that they name: The 2 owners of one query span differ. Among the rows of one device no owner is named more than 2 times.
All inputs are finite; a program needn't handle non-finite values.
Results may differ from the reference program's by a relative error of at most 0.02.
The reference program's roundings to bfloat16 on the way count: a program that leaves them out, or rounds other values in their place, can miss the bound.
Values may be sent and summed in bfloat16 or wider, within the bound.
A program may use at most 128 MiB of HBM per device.

```python
import math
import jax
import jax.numpy as jnp
import numpy as np
from jax import lax

E = 1536
DH = 128
CT = 64
NT = 64
K = 2
CPD = 4
DB_DEV = 12
CAP = 2
SPANS = 512
TOKENS = 32768
DBROWS = 384
N_SHARD = 32


def draw_queries(key, part):
    key = jax.random.fold_in(key, 3)
    first = jax.random.fold_in(key, 0)
    return jnp.clip(jax.random.normal(first, (TOKENS, E), jnp.float32), -6.0, 6.0).astype(jnp.bfloat16)


def draw_database(key, part):
    key = jax.random.fold_in(key, 5)
    return jnp.clip(jax.random.normal(key, (DBROWS, NT, E), jnp.float32), -6.0, 6.0).astype(jnp.bfloat16)


def draw_ctx_keys(key, part):
    key = jax.random.fold_in(key, 7)
    first = jax.random.fold_in(key, 0)
    return jnp.clip(jax.random.normal(first, (TOKENS, E), jnp.float32), -6.0, 6.0).astype(jnp.bfloat16)


def place_ends(drawn, key, least, high):
    spot = [jax.random.randint(jax.random.fold_in(key, axis), (), 0, length) for axis, length in enumerate(drawn.shape)]
    longest = drawn.shape.index(max(drawn.shape))
    neighbour = spot[:longest] + [(spot[longest] + 1) % drawn.shape[longest]] + spot[longest + 1:]
    return drawn.at[tuple(spot)].set(least).at[tuple(neighbour)].set(high)


def steps_of(key, extent, pieces, smallest, high):
    level = 1.0
    for dim, parts in pieces:
        heights = jax.random.uniform(jax.random.fold_in(jax.random.fold_in(key, 6), dim), (parts,), jnp.float32, smallest / len(pieces), high / len(pieces))
        level = level * jnp.repeat(jnp.exp(heights), extent[dim] // parts).reshape((-1,) + (1,) * (len(extent) - 1 - dim))
    return level


def shared_out(rng, own, number, rows, count, top, bound, lean):
    ranking = jax.random.permutation(rng, count)
    packed, common = portions_of(count, rows * top, bound, lean, True), portions_of(count, rows * top, bound, lean, False)
    places = jnp.arange(count)

    def named(sizes, offset_by):
        used = int((sizes > 0).sum())
        fixed = max(1, used // 4)
        shifted = fixed + (places - fixed + offset_by * (used - fixed)) % max(1, count - fixed)
        return jnp.zeros((count,), jnp.int32).at[ranking[jnp.where(places < fixed, places, shifted)]].set(jnp.asarray(sizes, jnp.int32))

    sizes = jnp.where(number % 4 == 0, named(packed, number // 4), named(common, number - number // 4 - 1))
    mixed = jax.random.permutation(jax.random.fold_in(own, 3), count)
    donor, taker = mixed[0:count // 2 * 2:2], mixed[1:count // 2 * 2:2]
    margin = jnp.minimum(sizes[donor] - 1, bound - sizes[taker]) // 2
    margin = jnp.where((donor == ranking[0]) | (taker == ranking[0]) | (sizes[taker] == 0), 0, jnp.maximum(margin, 0))
    shifted = jax.random.randint(jax.random.fold_in(own, 4), (count // 2,), 0, 1 << 20) % (margin + 1)
    sizes = sizes.at[donor].add(-shifted).at[taker].add(shifted)
    labels = jnp.searchsorted(jnp.cumsum(sizes), jnp.arange(rows * top), side="right").astype(jnp.int32)
    grid = labels.reshape(top, rows).T
    grid = grid[jax.random.permutation(jax.random.fold_in(own, 1), rows)]
    offset_by = jax.random.randint(jax.random.fold_in(own, 2), (rows, 1), 0, top)
    return jnp.take_along_axis(grid, (jnp.arange(top)[None, :] + offset_by) % top, axis=1)


def portions_of(amount, total, bound, slope, full):
    portions = [(1 << 20) // math.isqrt(rank ** slope) + 1 for rank in range(1, amount + 1)]
    largest = bound if full else min(bound, max(-(-total // amount), total * portions[0] // sum(portions)))
    least = 1 if total - largest >= amount - 1 else 0
    counts, surplus = [largest] + [least] * (amount - 1), total - largest - least * (amount - 1)
    while surplus > 0:
        candidates = [i for i in range(1, amount) if counts[i] < largest] or [i for i in range(1, amount) if counts[i] < bound]
        mass, remaining = sum([portions[i] for i in candidates]), surplus
        for i in candidates:
            more = min(bound - counts[i], max(1, remaining * portions[i] // mass), surplus)
            counts[i] = counts[i] + more
            surplus = surplus - more
    return np.array(counts)


def normal_values(own_key, shape, width, most, shards=(), kind=jnp.bfloat16):
    gain = steps_of(own_key, shape, shards, -0.22, 0.18) if shards else 1.0
    result = jax.random.normal(own_key, shape, jnp.float32) * width * gain
    return jnp.minimum(jnp.maximum(result, -most), most).astype(kind)


def setup_inputs(seed: int = 0) -> dict:
    arg_keys = jax.random.split(jax.random.key(seed), 11)
    queries = draw_queries(jax.random.fold_in(arg_keys[10], 71), 0)
    ctx_keys = draw_ctx_keys(jax.random.fold_in(arg_keys[10], 71), 0)
    ctx_values = normal_values(arg_keys[2], (TOKENS, E), 1.0, 6.0, ((0, 128), (1, 2)))
    cotangent = normal_values(arg_keys[3], (TOKENS, E), 1.0, 6.0, ((0, 128), (1, 2)))
    owner_keys = jax.random.split(jax.random.fold_in(arg_keys[4], 1), SPANS // CPD)
    owner_turns = jax.random.permutation(jax.random.fold_in(arg_keys[4], 3), SPANS // CPD)
    owner = jax.vmap(lambda own, number: shared_out(jax.random.fold_in(arg_keys[4], 2), own, number, CPD, N_SHARD, K, CAP, 2))(owner_keys, owner_turns).reshape((SPANS, K))
    slot_row = place_ends(jax.random.randint(arg_keys[5], (SPANS, K), 0, DB_DEV), jax.random.fold_in(arg_keys[5], 1), 0, DB_DEV - 1).astype(jnp.int32)
    database = draw_database(jax.random.fold_in(arg_keys[10], 71), 0)
    enc_gain = jnp.clip(1.0 + 0.15 * jax.random.normal(arg_keys[7], (E,), jnp.float32), 0.25, 1.75)
    enc_query_w = normal_values(arg_keys[8], (E, E), E ** -0.5, 0.15625, ((0, 4), (1, 2)))
    enc_out_w = normal_values(arg_keys[9], (E, E), E ** -0.5, 0.15625, ((0, 4), (1, 2)))
    return dict(queries=queries, ctx_keys=ctx_keys, ctx_values=ctx_values, cotangent=cotangent, owner=owner, slot_row=slot_row, database=database, enc_gain=enc_gain, enc_query_w=enc_query_w, enc_out_w=enc_out_w)


def softmax_rows(scores):
    top = lax.optimization_barrier(jnp.max(scores, axis=-1, keepdims=True))
    weights = jnp.exp(scores - top)
    return weights / lax.optimization_barrier(jnp.sum(weights, axis=-1, keepdims=True))

def rounded(values):
    return lax.optimization_barrier(values.astype(jnp.bfloat16)).astype(jnp.float32)

def block_pass(items, database, enc_gain, enc_query_w, enc_out_w):
    queries, ctx_keys, ctx_values, cotangent, owner, slot_row = items
    blocks = owner.shape[0]
    heads = E // DH
    scale = DH ** (-0.5)
    index = (owner * DB_DEV + slot_row).reshape(-1).astype(jnp.int32)
    fetched = jnp.take(database, index, axis=0)
    wide = fetched.reshape(-1, E).astype(jnp.float32)
    squares = lax.optimization_barrier(jnp.mean(wide * wide, axis=1, keepdims=True))
    normed = (wide * lax.rsqrt(squares + 1e-06) * enc_gain).astype(jnp.bfloat16)
    enc_q = jnp.dot(normed, enc_query_w, preferred_element_type=jnp.float32).astype(jnp.bfloat16)
    enc_q4 = enc_q.reshape(blocks, K * NT, heads, DH).astype(jnp.float32)
    keys4 = ctx_keys.reshape(blocks, CT, heads, DH).astype(jnp.float32)
    values4 = ctx_values.reshape(blocks, CT, heads, DH).astype(jnp.float32)
    enc_p = softmax_rows(jnp.einsum('cqhd,ckhd->chqk', enc_q4, keys4) * scale)
    enc_pb = rounded(enc_p)
    mixed = jnp.einsum('chqk,ckhd->cqhd', enc_pb, values4).astype(jnp.bfloat16)
    projected = jnp.dot(mixed.reshape(-1, E), enc_out_w.T, preferred_element_type=jnp.float32)
    encoded = (wide + projected).astype(jnp.bfloat16)
    enc4 = encoded.reshape(blocks, K * NT, heads, DH).astype(jnp.float32)
    query4 = queries.reshape(blocks, CT, heads, DH).astype(jnp.float32)
    cca_p = softmax_rows(jnp.einsum('cqhd,ckhd->chqk', query4, enc4) * scale)
    cca_pb = rounded(cca_p)
    attended = jnp.einsum('chqk,ckhd->cqhd', cca_pb, enc4).astype(jnp.bfloat16)
    grad4 = cotangent.reshape(blocks, CT, heads, DH).astype(jnp.float32)
    d_p = jnp.einsum('cqhd,ckhd->chqk', grad4, enc4)
    d_s = rounded(cca_p * (d_p - lax.optimization_barrier(jnp.sum(d_p * cca_p, axis=-1, keepdims=True))))
    grad_queries = (scale * jnp.einsum('chqk,ckhd->cqhd', d_s, enc4)).astype(jnp.bfloat16)
    d_enc = (scale * jnp.einsum('chqk,cqhd->ckhd', d_s, query4) + jnp.einsum('chqk,cqhd->ckhd', cca_pb, grad4)).astype(jnp.bfloat16)
    d_mixed = jnp.dot(d_enc.reshape(-1, E), enc_out_w, preferred_element_type=jnp.float32).astype(jnp.bfloat16)
    d_mixed4 = d_mixed.reshape(blocks, K * NT, heads, DH).astype(jnp.float32)
    grad_values = jnp.einsum('chqk,cqhd->ckhd', enc_pb, d_mixed4).astype(jnp.bfloat16)
    d_pe = jnp.einsum('cqhd,ckhd->chqk', d_mixed4, values4)
    d_se = rounded(enc_p * (d_pe - lax.optimization_barrier(jnp.sum(d_pe * enc_p, axis=-1, keepdims=True))))
    grad_keys = (scale * jnp.einsum('chqk,cqhd->ckhd', d_se, enc_q4)).astype(jnp.bfloat16)
    shape = (blocks * CT, E)
    return (attended.reshape(shape), grad_queries.reshape(shape), grad_keys.reshape(shape), grad_values.reshape(shape))

def reference(queries, ctx_keys, ctx_values, cotangent, owner, slot_row, database, enc_gain, enc_query_w, enc_out_w):
    groups = SPANS // CPD
    items = (queries.reshape(groups, CPD * CT, E), ctx_keys.reshape(groups, CPD * CT, E), ctx_values.reshape(groups, CPD * CT, E), cotangent.reshape(groups, CPD * CT, E), owner.reshape(groups, CPD, K), slot_row.reshape(groups, CPD, K))
    results = lax.map(lambda one: block_pass(one, database, enc_gain, enc_query_w, enc_out_w), items)
    attended, grad_queries, grad_keys, grad_values = results
    return (attended.reshape(TOKENS, E), grad_queries.reshape(TOKENS, E), grad_keys.reshape(TOKENS, E), grad_values.reshape(TOKENS, E))
```

```python
import jax
import jax.numpy as jnp
from jax import lax
from jax.experimental import pallas as pl
from jax.experimental.pallas import tpu as pltpu
from jax.sharding import PartitionSpec as P

DH = 128
CT = 64
NT = 64
K = 2
MESH = pl.DeviceIdType.MESH


def fetch_kernel(req_ref, db_ref, out_ref, rq, rqs, gath, xs, xr, xm,
                 loc_sem, rq_send, rq_recv, rx_send, rx_recv, sib_send, sib_recv,
                 zp_send, zp_recv, zm_send, zm_recv, x_send, x_recv, y_send, y_recv, m_send, m_recv):
    s = lax.axis_index("section")
    d = lax.axis_index("shard")
    m = lax.axis_index("mp")
    x = d // 16
    z = (d // 2) % 8
    c = d % 2

    def dev(s_, x_, z_, c_, m_):
        return (s_, x_ * 16 + z_ * 2 + c_, m_)

    peers = [(ds, dc) for ds in (2, 1, 3, 0) for dc in (0, 1) if (ds, dc) != (0, 0)]
    zn, zb = (z + 1) % 8, (z + 7) % 8

    def peer(ds, dc):
        return dev((s + ds) % 4, x, z, (c + dc) % 2, m)

    pair = dev(s, 1 - x, z, c, m)
    up, down = dev(s, x, zn, c, m), dev(s, x, zb, c, m)
    mate = dev(s, x, z, c, 1 - m)
    sib = dev(s, x, z, 1 - c, m)

    barrier = pltpu.get_barrier_semaphore()
    friends = [peer(*p) for p in peers] + [pair, up, down, mate]
    for f in friends:
        pl.semaphore_signal(barrier, inc=1, device_id=f, device_id_type=MESH)

    tok = pl.ds(pl.multiple_of(s * 16, 16), 16)
    mine = pltpu.make_async_copy(
        db_ref.at[:, tok, pl.ds(pl.multiple_of((2 * m + c) * 384, 128), 384)],
        gath.at[pl.ds(z * 24 + c * 12, 12)], loc_sem.at[0])
    mine.start()
    me = s * 2 + c
    own_rq = pltpu.make_async_copy(req_ref, rq.at[x * 8 + me], loc_sem.at[1])
    own_rq.start()
    pl.semaphore_wait(barrier, len(friends))

    to_sib = pltpu.make_async_remote_copy(
        db_ref.at[:, tok, pl.ds(pl.multiple_of((2 * m + 1 - c) * 384, 128), 384)],
        gath.at[pl.ds(z * 24 + c * 12, 12)], sib_send.at[0], sib_recv.at[0],
        device_id=sib, device_id_type=MESH)
    to_sib.start()
    rq_copies = []
    for i, (ds, dc) in enumerate(peers):
        src = ((s + 4 - ds) % 4) * 2 + (c + dc) % 2
        cp = pltpu.make_async_remote_copy(
            req_ref, rq.at[x * 8 + me], rq_send.at[i], rq_recv.at[i],
            device_id=peer(ds, dc), device_id_type=MESH)
        cp.start()
        rq_copies.append(cp)

    def zcopy(j, plus):
        k, h = j // 2, j % 2
        if k == 3:
            h = 0 if plus else 1
        zz = (z + 8 - k) % 8 if plus else (z + k) % 8
        cls = (c + h) % 2
        sl = gath.at[pl.ds(zz * 24 + cls * 12, 12)]
        return pltpu.make_async_remote_copy(
            sl, sl, (zp_send if plus else zm_send).at[j], (zp_recv if plus else zm_recv).at[j],
            device_id=up if plus else down, device_id_type=MESH)

    plus, minus = [], []
    for j in range(7):
        if j == 0:
            mine.wait()
        elif j == 1:
            to_sib.wait_recv()
        elif j < 6:
            plus[j - 2].wait_recv()
            minus[j - 2].wait_recv()
        else:
            plus[4].wait_recv()
            minus[5].wait_recv()
        a, b = zcopy(j, True), zcopy(j, False)
        a.start()
        b.start()
        plus.append(a)
        minus.append(b)
        if j == 2:
            own_rq.wait()
            for cp in rq_copies:
                cp.wait_recv()
            fwd = pltpu.make_async_remote_copy(
                rq.at[pl.ds(x * 8, 8)], rq.at[pl.ds(x * 8, 8)], rx_send.at[0], rx_recv.at[0],
                device_id=pair, device_id_type=MESH)
            fwd.start()
        if j == 4:
            fwd.wait_recv()
            to_s = pltpu.make_async_copy(rq, rqs, loc_sem.at[2])
            to_s.start()
            to_s.wait()
    plus[5].wait_recv()
    plus[6].wait_recv()
    minus[4].wait_recv()
    minus[6].wait_recv()

    order = [(ds, dc) for ds in (2, 1, 3, 0) for dc in (0, 1)]
    xcopies = []
    for i, (ds, dc) in enumerate(order):
        dst = ((s + ds) % 4) * 2 + (c + dc) % 2
        for j in range(8):
            g = rqs[(1 - x) * 8 + dst, 0, j]
            xs[i * 8 + j] = gath[lax.rem(g, 192)]
        cp = pltpu.make_async_remote_copy(
            xs.at[pl.ds(i * 8, 8)], xr.at[pl.ds(i * 8, 8)], x_send.at[i], x_recv.at[i],
            device_id=pair, device_id_type=MESH)
        cp.start()
        xcopies.append(cp)
    ycopies = []
    feat = pl.ds(pl.multiple_of((2 * m + c) * 384, 128), 384)
    for i, (ds, dc) in enumerate(order):
        dst = ((s + ds) % 4) * 2 + (c + dc) % 2
        xcopies[i].wait_recv()
        for j in range(8):
            g = rqs[x * 8 + dst, 0, j]
            own = (g // 192) == x
            xm[i * 8 + j] = jnp.where(own, gath[lax.rem(g, 192)], xr[i * 8 + j])
        if (ds, dc) == (0, 0):
            cp = pltpu.make_async_copy(xm.at[pl.ds(i * 8, 8)], out_ref.at[:, tok, feat], y_recv.at[i])
        else:
            cp = pltpu.make_async_remote_copy(
                xm.at[pl.ds(i * 8, 8)], out_ref.at[:, tok, feat], y_send.at[i], y_recv.at[i],
                device_id=peer(ds, dc), device_id_type=MESH)
        cp.start()
        ycopies.append(cp)
    mcopies = []
    for i, (ds, dc) in enumerate(order):
        if (ds, dc) == (0, 0):
            ycopies[i].wait()
        else:
            ycopies[i].wait_recv()
        ss, cc = (s + 4 - ds) % 4, (c + dc) % 2
        piece = out_ref.at[:, pl.ds(pl.multiple_of(ss * 16, 16), 16),
                           pl.ds(pl.multiple_of((2 * m + cc) * 384, 128), 384)]
        cp = pltpu.make_async_remote_copy(piece, piece, m_send.at[i], m_recv.at[i],
                                          device_id=mate, device_id_type=MESH)
        cp.start()
        mcopies.append(cp)
    for cp in mcopies:
        cp.wait_recv()
    to_sib.wait_send()
    fwd.wait_send()
    for cp in rq_copies + plus + minus + xcopies + mcopies:
        cp.wait_send()
    for i, p in enumerate(order):
        if p != (0, 0):
            ycopies[i].wait_send()


def fetch(req, database):
    dma = pltpu.SemaphoreType.DMA
    bf = jnp.bfloat16
    return pl.pallas_call(
        fetch_kernel,
        out_shape=jax.ShapeDtypeStruct((8, 64, 1536), bf),
        in_specs=[pl.BlockSpec(memory_space=pltpu.VMEM), pl.BlockSpec(memory_space=pl.ANY)],
        out_specs=pl.BlockSpec(memory_space=pltpu.VMEM),
        scratch_shapes=[
            pltpu.VMEM((16, 8, 128), jnp.int32),
            pltpu.SMEM((16, 8, 128), jnp.int32),
            pltpu.VMEM((192, 16, 384), bf),
            pltpu.VMEM((64, 16, 384), bf),
            pltpu.VMEM((64, 16, 384), bf),
            pltpu.VMEM((64, 16, 384), bf),
            dma((3,)),
            dma((7,)), dma((7,)), dma((1,)), dma((1,)), dma((1,)), dma((1,)),
            dma((7,)), dma((7,)), dma((7,)), dma((7,)),
            dma((8,)), dma((8,)), dma((8,)), dma((8,)), dma((8,)), dma((8,)),
        ],
        compiler_params=pltpu.CompilerParams(
            collective_id=0, has_side_effects=True, vmem_limit_bytes=32 * 1024 * 1024),
        cost_estimate=pl.CostEstimate(flops=0, bytes_accessed=12_000_000, transcendentals=0),
    )(req, database)


def softmax_rows(scores):
    top = jnp.max(scores, axis=-1, keepdims=True)
    weights = jnp.exp(scores - top)
    return weights / jnp.sum(weights, axis=-1, keepdims=True)


def local(
    queries,
    ctx_keys,
    ctx_values,
    cotangent,
    owner,
    slot_row,
    database,
    enc_gain,
    enc_query_w,
    enc_out_w,
):
    half = queries.shape[1]
    width = database.shape[2]
    heads = half // DH
    blocks = owner.shape[0]
    scale = DH ** (-0.5)
    part = lax.axis_index("mp")
    wanted = (owner * database.shape[0] + slot_row).reshape(1, -1)
    request = jnp.pad(wanted, ((0, 7), (0, 128 - wanted.shape[1])))
    fetched = fetch(request, database)
    wide = fetched.reshape(-1, width).astype(jnp.float32)
    squares = jnp.mean(wide * wide, axis=1, keepdims=True)
    normed = (wide * lax.rsqrt(squares + 1e-06) * enc_gain).astype(jnp.bfloat16)
    query_full, out_full = (
        lax.all_gather(enc_query_w, "section", axis=0, tiled=True),
        lax.all_gather(enc_out_w, "section", axis=0, tiled=True),
    )
    enc_q = jnp.dot(normed, query_full, preferred_element_type=jnp.float32).astype(jnp.bfloat16)
    enc_q4 = enc_q.reshape(blocks, K * NT, heads, DH)
    keys4 = ctx_keys.reshape(blocks, CT, heads, DH)
    values4 = ctx_values.reshape(blocks, CT, heads, DH)
    enc_p = softmax_rows(
        jnp.einsum("cqhd,ckhd->chqk", enc_q4, keys4, preferred_element_type=jnp.float32) * scale
    )
    enc_pb = enc_p.astype(jnp.bfloat16)
    mixed = jnp.einsum(
        "chqk,ckhd->cqhd", enc_pb, values4, preferred_element_type=jnp.float32
    ).astype(jnp.bfloat16)
    projected = lax.dot_general(
        mixed.reshape(-1, half),
        out_full,
        (((1,), (1,)), ((), ())),
        preferred_element_type=jnp.float32,
    )
    own_sum = lax.psum_scatter(projected, "mp", scatter_dimension=1, tiled=True)
    residual = lax.dynamic_slice_in_dim(wide, part * half, half, 1)
    encoded = (residual + own_sum).astype(jnp.bfloat16)
    enc4 = encoded.reshape(blocks, K * NT, heads, DH)
    query4 = queries.reshape(blocks, CT, heads, DH)
    cca_p = softmax_rows(
        jnp.einsum("cqhd,ckhd->chqk", query4, enc4, preferred_element_type=jnp.float32) * scale
    )
    cca_pb = cca_p.astype(jnp.bfloat16)
    attended = jnp.einsum(
        "chqk,ckhd->cqhd", cca_pb, enc4, preferred_element_type=jnp.float32
    ).astype(jnp.bfloat16)
    grad4 = cotangent.reshape(blocks, CT, heads, DH)
    d_p = jnp.einsum("cqhd,ckhd->chqk", grad4, enc4, preferred_element_type=jnp.float32)
    d_s = (cca_p * (d_p - jnp.sum(d_p * cca_p, axis=-1, keepdims=True))).astype(jnp.bfloat16)
    grad_queries = (
        scale * jnp.einsum("chqk,ckhd->cqhd", d_s, enc4, preferred_element_type=jnp.float32)
    ).astype(jnp.bfloat16)
    key_part = jnp.einsum("chqk,cqhd->ckhd", d_s, query4, preferred_element_type=jnp.float32)
    value_part = jnp.einsum("chqk,cqhd->ckhd", cca_pb, grad4, preferred_element_type=jnp.float32)
    d_enc = (scale * key_part + value_part).astype(jnp.bfloat16)
    d_full = lax.all_gather(d_enc.reshape(-1, half), "mp", axis=1, tiled=True)
    d_mixed = jnp.dot(d_full, out_full, preferred_element_type=jnp.float32).astype(jnp.bfloat16)
    d_mixed4 = d_mixed.reshape(blocks, K * NT, heads, DH)
    grad_values = jnp.einsum(
        "chqk,cqhd->ckhd", enc_pb, d_mixed4, preferred_element_type=jnp.float32
    ).astype(jnp.bfloat16)
    d_pe = jnp.einsum("cqhd,ckhd->chqk", d_mixed4, values4, preferred_element_type=jnp.float32)
    d_se = (enc_p * (d_pe - jnp.sum(d_pe * enc_p, axis=-1, keepdims=True))).astype(jnp.bfloat16)
    grad_keys = (
        scale * jnp.einsum("chqk,cqhd->ckhd", d_se, enc_q4, preferred_element_type=jnp.float32)
    ).astype(jnp.bfloat16)
    shape = (blocks * CT, half)
    return (
        attended.reshape(shape),
        grad_queries.reshape(shape),
        grad_keys.reshape(shape),
        grad_values.reshape(shape),
    )


def solution(mesh):
    return jax.shard_map(
        local,
        mesh=mesh,
        in_specs=(
            P(("section", "shard"), "mp"),
            P(("section", "shard"), "mp"),
            P(("section", "shard"), "mp"),
            P(("section", "shard"), "mp"),
            P(("section", "shard"), None),
            P(("section", "shard"), None),
            P("shard", None, None),
            P(),
            P("section", "mp"),
            P("section", "mp"),
        ),
        out_specs=(
            P(("section", "shard"), "mp"),
            P(("section", "shard"), "mp"),
            P(("section", "shard"), "mp"),
            P(("section", "shard"), "mp"),
        ),
        check_vma=False,
    )
```

```python
import jax
import jax.numpy as jnp
from jax import lax
from jax.experimental import pallas as pl
from jax.experimental.pallas import tpu as pltpu
from jax.sharding import PartitionSpec as P

DH = 128
CT = 64
NT = 64
K = 2
MESH = pl.DeviceIdType.MESH


def fetch_kernel(req_ref, db_ref, out_ref, rq, rqs, gath, xs, xr, xm,
                 loc_sem, rq_send, rq_recv, rx_send, rx_recv, sib_send, sib_recv,
                 zp_send, zp_recv, zm_send, zm_recv, x_send, x_recv, y_send, y_recv, m_send, m_recv):
    s = lax.axis_index("section")
    d = lax.axis_index("shard")
    m = lax.axis_index("mp")
    x = d // 16
    z = (d // 2) % 8
    c = d % 2

    def dev(s_, x_, z_, c_, m_):
        return (s_, x_ * 16 + z_ * 2 + c_, m_)

    peers = [(ds, dc) for ds in (2, 1, 3, 0) for dc in (0, 1) if (ds, dc) != (0, 0)]
    zn, zb = (z + 1) % 8, (z + 7) % 8

    def peer(ds, dc):
        return dev((s + ds) % 4, x, z, (c + dc) % 2, m)

    pair = dev(s, 1 - x, z, c, m)
    up, down = dev(s, x, zn, c, m), dev(s, x, zb, c, m)
    mate = dev(s, x, z, c, 1 - m)
    sib = dev(s, x, z, 1 - c, m)

    barrier = pltpu.get_barrier_semaphore()
    friends = [peer(*p) for p in peers] + [pair, up, down, mate]
    for f in friends:
        pl.semaphore_signal(barrier, inc=1, device_id=f, device_id_type=MESH)

    tok = pl.ds(pl.multiple_of(s * 16, 16), 16)
    mine = pltpu.make_async_copy(
        db_ref.at[:, tok, pl.ds(pl.multiple_of((2 * m + c) * 384, 128), 384)],
        gath.at[pl.ds(z * 24 + c * 12, 12)], loc_sem.at[0])
    mine.start()
    me = s * 2 + c
    own_rq = pltpu.make_async_copy(req_ref, rq.at[x * 8 + me], loc_sem.at[1])
    own_rq.start()
    pl.semaphore_wait(barrier, len(friends))

    to_sib = pltpu.make_async_remote_copy(
        db_ref.at[:, tok, pl.ds(pl.multiple_of((2 * m + 1 - c) * 384, 128), 384)],
        gath.at[pl.ds(z * 24 + c * 12, 12)], sib_send.at[0], sib_recv.at[0],
        device_id=sib, device_id_type=MESH)
    to_sib.start()
    rq_copies = []
    for i, (ds, dc) in enumerate(peers):
        src = ((s + 4 - ds) % 4) * 2 + (c + dc) % 2
        cp = pltpu.make_async_remote_copy(
            req_ref, rq.at[x * 8 + me], rq_send.at[i], rq_recv.at[i],
            device_id=peer(ds, dc), device_id_type=MESH)
        cp.start()
        rq_copies.append(cp)

    def zcopy(j, plus):
        k, h = j // 2, j % 2
        if k == 3:
            h = 0 if plus else 1
        zz = (z + 8 - k) % 8 if plus else (z + k) % 8
        cls = (c + h) % 2
        sl = gath.at[pl.ds(zz * 24 + cls * 12, 12)]
        return pltpu.make_async_remote_copy(
            sl, sl, (zp_send if plus else zm_send).at[j], (zp_recv if plus else zm_recv).at[j],
            device_id=up if plus else down, device_id_type=MESH)

    plus, minus = [], []
    for j in range(7):
        if j == 0:
            mine.wait()
        elif j == 1:
            to_sib.wait_recv()
        elif j < 6:
            plus[j - 2].wait_recv()
            minus[j - 2].wait_recv()
        else:
            plus[4].wait_recv()
            minus[5].wait_recv()
        a, b = zcopy(j, True), zcopy(j, False)
        a.start()
        b.start()
        plus.append(a)
        minus.append(b)
        if j == 2:
            own_rq.wait()
            for cp in rq_copies:
                cp.wait_recv()
            fwd = pltpu.make_async_remote_copy(
                rq.at[pl.ds(x * 8, 8)], rq.at[pl.ds(x * 8, 8)], rx_send.at[0], rx_recv.at[0],
                device_id=pair, device_id_type=MESH)
            fwd.start()
        if j == 4:
            fwd.wait_recv()
            to_s = pltpu.make_async_copy(rq, rqs, loc_sem.at[2])
            to_s.start()
            to_s.wait()
    plus[5].wait_recv()
    plus[6].wait_recv()
    minus[4].wait_recv()
    minus[6].wait_recv()

    order = [(ds, dc) for ds in (2, 1, 3, 0) for dc in (0, 1)]
    xcopies = []
    for i, (ds, dc) in enumerate(order):
        dst = ((s + ds) % 4) * 2 + (c + dc) % 2
        for j in range(8):
            g = rqs[(1 - x) * 8 + dst, 0, j]
            xs[i * 8 + j] = gath[lax.rem(g, 192)]
        cp = pltpu.make_async_remote_copy(
            xs.at[pl.ds(i * 8, 8)], xr.at[pl.ds(i * 8, 8)], x_send.at[i], x_recv.at[i],
            device_id=pair, device_id_type=MESH)
        cp.start()
        xcopies.append(cp)
    ycopies = []
    feat = pl.ds(pl.multiple_of((2 * m + c) * 384, 128), 384)
    for i, (ds, dc) in enumerate(order):
        dst = ((s + ds) % 4) * 2 + (c + dc) % 2
        xcopies[i].wait_recv()
        for j in range(8):
            g = rqs[x * 8 + dst, 0, j]
            own = (g // 192) == x
            xm[i * 8 + j] = jnp.where(own, gath[lax.rem(g, 192)], xr[i * 8 + j])
        if (ds, dc) == (0, 0):
            cp = pltpu.make_async_copy(xm.at[pl.ds(i * 8, 8)], out_ref.at[:, tok, feat], y_recv.at[i])
        else:
            cp = pltpu.make_async_remote_copy(
                xm.at[pl.ds(i * 8, 8)], out_ref.at[:, tok, feat], y_send.at[i], y_recv.at[i],
                device_id=peer(ds, dc), device_id_type=MESH)
        cp.start()
        ycopies.append(cp)
    mcopies = []
    for i, (ds, dc) in enumerate(order):
        if (ds, dc) == (0, 0):
            ycopies[i].wait()
        else:
            ycopies[i].wait_recv()
        ss, cc = (s + 4 - ds) % 4, (c + dc) % 2
        piece = out_ref.at[:, pl.ds(pl.multiple_of(ss * 16, 16), 16),
                           pl.ds(pl.multiple_of((2 * m + cc) * 384, 128), 384)]
        cp = pltpu.make_async_remote_copy(piece, piece, m_send.at[i], m_recv.at[i],
                                          device_id=mate, device_id_type=MESH)
        cp.start()
        mcopies.append(cp)
    for cp in mcopies:
        cp.wait_recv()
    to_sib.wait_send()
    fwd.wait_send()
    for cp in rq_copies + plus + minus + xcopies + mcopies:
        cp.wait_send()
    for i, p in enumerate(order):
        if p != (0, 0):
            ycopies[i].wait_send()


def fetch(req, database):
    dma = pltpu.SemaphoreType.DMA
    bf = jnp.bfloat16
    return pl.pallas_call(
        fetch_kernel,
        out_shape=jax.ShapeDtypeStruct((8, 64, 1536), bf),
        in_specs=[pl.BlockSpec(memory_space=pltpu.VMEM), pl.BlockSpec(memory_space=pl.ANY)],
        out_specs=pl.BlockSpec(memory_space=pltpu.VMEM),
        scratch_shapes=[
            pltpu.VMEM((16, 8, 128), jnp.int32),
            pltpu.SMEM((16, 8, 128), jnp.int32),
            pltpu.VMEM((192, 16, 384), bf),
            pltpu.VMEM((64, 16, 384), bf),
            pltpu.VMEM((64, 16, 384), bf),
            pltpu.VMEM((64, 16, 384), bf),
            dma((3,)),
            dma((7,)), dma((7,)), dma((1,)), dma((1,)), dma((1,)), dma((1,)),
            dma((7,)), dma((7,)), dma((7,)), dma((7,)),
            dma((8,)), dma((8,)), dma((8,)), dma((8,)), dma((8,)), dma((8,)),
        ],
        compiler_params=pltpu.CompilerParams(
            collective_id=0, has_side_effects=True, vmem_limit_bytes=32 * 1024 * 1024),
        cost_estimate=pl.CostEstimate(flops=0, bytes_accessed=12_000_000, transcendentals=0),
    )(req, database)


def dot(a, b, dims):
    return lax.dot_general(a, b, (dims, ((), ())), preferred_element_type=jnp.float32)


AB = ((1,), (0,))
ABT = ((1,), (1,))
ATB = ((0,), (0,))


def block_kernel(f_ref, wq_ref, wo_ref, gain_ref, q_ref, k_ref, v_ref, t_ref,
                 att_ref, gq_ref, gk_ref, gv_ref,
                 encq, probs, mixed, part_own, part_out, part_in, denc, denc_in, dmix,
                 p_send, p_recv, d_send, d_recv):
    m = lax.axis_index("mp")
    mate = (lax.axis_index("section"), lax.axis_index("shard"), 1 - m)
    scale = DH ** (-0.5)
    f32, bf = jnp.float32, jnp.bfloat16
    heads = q_ref.shape[1] // DH
    half = heads * DH
    spans = q_ref.shape[0] // CT
    rows_n = K * NT
    own = pl.ds(pl.multiple_of(m * half, 128), half)
    other = pl.ds(pl.multiple_of((1 - m) * half, 128), half)
    barrier = pltpu.get_barrier_semaphore()
    pl.semaphore_signal(barrier, inc=1, device_id=mate, device_id_type=MESH)
    pl.semaphore_wait(barrier, 1)

    def send(src, dst, ss, rs, g):
        rows = pl.ds(pl.multiple_of(g * rows_n, rows_n), rows_n)
        return pltpu.make_async_remote_copy(
            src.at[rows], dst.at[rows], ss.at[g], rs.at[g], device_id=mate, device_id_type=MESH)

    def encode(g, _):
        rows = pl.ds(pl.multiple_of(g * rows_n, rows_n), rows_n)
        toks = pl.ds(pl.multiple_of(g * CT, CT), CT)
        wide = f_ref[rows, :].astype(f32)
        mean = jnp.mean(wide * wide, axis=1, keepdims=True)
        normed = (wide * lax.rsqrt(mean + 1e-06) * gain_ref[...]).astype(bf)
        encq[rows, :] = dot(normed, wq_ref[...], AB).astype(bf)
        for h in range(heads):
            cols = slice(h * DH, (h + 1) * DH)
            st = dot(k_ref[toks, cols], encq[rows, cols], ABT) * scale
            e = jnp.exp(st - jnp.max(st, axis=0, keepdims=True))
            p = e / jnp.sum(e, axis=0, keepdims=True)
            probs[g * heads + h] = p
            mixed[:, cols] = dot(p.astype(bf), v_ref[toks, cols], ATB).astype(bf)
        part_out[rows, :] = dot(mixed[...], wo_ref[other, :], ABT).astype(bf)
        send(part_out, part_in, p_send, p_recv, g).start()
        part_own[rows, :] = dot(mixed[...], wo_ref[own, :], ABT)
        return 0

    def cross(g, _):
        rows = pl.ds(pl.multiple_of(g * rows_n, rows_n), rows_n)
        toks = pl.ds(pl.multiple_of(g * CT, CT), CT)
        send(part_out, part_in, p_send, p_recv, g).wait()
        for h in range(heads):
            cols = slice(h * DH, (h + 1) * DH)
            raw = f_ref[rows, pl.ds(pl.multiple_of(m * half + h * DH, 128), DH)].astype(f32)
            enc = (raw + (part_own[rows, cols] + part_in[rows, cols].astype(f32))).astype(bf)
            q, t = q_ref[toks, cols], t_ref[toks, cols]
            both = dot(jnp.concatenate([q, t], axis=0), enc, ABT)
            s, dp = both[:CT] * scale, both[CT:]
            e = jnp.exp(s - jnp.max(s, axis=1, keepdims=True))
            p = e / jnp.sum(e, axis=1, keepdims=True)
            pb = p.astype(bf)
            ds = (p * (dp - jnp.sum(dp * p, axis=1, keepdims=True))).astype(bf)
            out = dot(jnp.concatenate([pb, ds], axis=0), enc, AB)
            att_ref[toks, cols] = out[:CT].astype(bf)
            gq_ref[toks, cols] = (scale * out[CT:]).astype(bf)
            denc[rows, cols] = (scale * dot(ds, q, ATB) + dot(pb, t, ATB)).astype(bf)
        send(denc, denc_in, d_send, d_recv, g).start()
        return 0

    def back(g, _):
        rows = pl.ds(pl.multiple_of(g * rows_n, rows_n), rows_n)
        toks = pl.ds(pl.multiple_of(g * CT, CT), CT)
        near = dot(denc[rows, :], wo_ref[own, :], AB)
        send(denc, denc_in, d_send, d_recv, g).wait()
        dmix[...] = (near + dot(denc_in[rows, :], wo_ref[other, :], AB)).astype(bf)
        for h in range(heads):
            cols = slice(h * DH, (h + 1) * DH)
            p = probs[g * heads + h]
            dm = dmix[:, cols]
            gv_ref[toks, cols] = dot(p.astype(bf), dm, AB).astype(bf)
            dpe = dot(v_ref[toks, cols], dm, ABT)
            dse = (p * (dpe - jnp.sum(dpe * p, axis=0, keepdims=True))).astype(bf)
            gk_ref[toks, cols] = (scale * dot(dse, encq[rows, cols], AB)).astype(bf)
        return 0

    lax.fori_loop(0, spans, encode, 0)
    lax.fori_loop(0, spans, cross, 0)
    lax.fori_loop(0, spans, back, 0)


def blocks_pass(fetched, wq, wo, gain, queries, keys, values, cotangent):
    dma = pltpu.SemaphoreType.DMA
    bf, f32 = jnp.bfloat16, jnp.float32
    tokens, half = queries.shape
    spans, heads = tokens // CT, half // DH
    rows = spans * K * NT
    out = jax.ShapeDtypeStruct((tokens, half), bf)
    vmem = pl.BlockSpec(memory_space=pltpu.VMEM)
    return pl.pallas_call(
        block_kernel,
        out_shape=(out,) * 4,
        in_specs=[vmem] * 8,
        out_specs=(vmem,) * 4,
        scratch_shapes=[
            pltpu.VMEM((rows, half), bf),
            pltpu.VMEM((spans * heads, CT, K * NT), f32),
            pltpu.VMEM((K * NT, half), bf),
            pltpu.VMEM((rows, half), f32),
            pltpu.VMEM((rows, half), bf),
            pltpu.VMEM((rows, half), bf),
            pltpu.VMEM((rows, half), bf),
            pltpu.VMEM((rows, half), bf),
            pltpu.VMEM((K * NT, half), bf),
            dma((spans,)), dma((spans,)), dma((spans,)), dma((spans,)),
        ],
        compiler_params=pltpu.CompilerParams(
            collective_id=1, has_side_effects=True, vmem_limit_bytes=40 * 1024 * 1024),
        cost_estimate=pl.CostEstimate(flops=4_600_000_000, bytes_accessed=12_000_000, transcendentals=600_000),
    )(fetched, wq, wo, gain, queries, keys, values, cotangent)


def local(queries, ctx_keys, ctx_values, cotangent, owner, slot_row, database, enc_gain, enc_query_w, enc_out_w):
    width = database.shape[2]
    wanted = (owner * database.shape[0] + slot_row).reshape(1, -1)
    request = jnp.pad(wanted, ((0, 7), (0, 128 - wanted.shape[1])))
    fetched = fetch(request, database).reshape(-1, width)
    query_full = lax.all_gather(enc_query_w, "section", axis=0, tiled=True)
    out_full = lax.all_gather(enc_out_w, "section", axis=0, tiled=True)
    return blocks_pass(
        fetched, query_full, out_full, enc_gain.reshape(1, -1), queries, ctx_keys, ctx_values, cotangent
    )


def solution(mesh):
    return jax.shard_map(
        local,
        mesh=mesh,
        in_specs=(
            P(("section", "shard"), "mp"),
            P(("section", "shard"), "mp"),
            P(("section", "shard"), "mp"),
            P(("section", "shard"), "mp"),
            P(("section", "shard"), None),
            P(("section", "shard"), None),
            P("shard", None, None),
            P(),
            P("section", "mp"),
            P("section", "mp"),
        ),
        out_specs=(
            P(("section", "shard"), "mp"),
            P(("section", "shard"), "mp"),
            P(("section", "shard"), "mp"),
            P(("section", "shard"), "mp"),
        ),
        check_vma=False,
    )
```

```python
import jax
import jax.numpy as jnp
from jax import lax
from jax.experimental import pallas as pl
from jax.experimental.pallas import tpu as pltpu
from jax.sharding import PartitionSpec as P

DH = 128
CT = 64
NT = 64
K = 2
DB = 12
SPANS = 4
REQ = SPANS * K
TOK = NT // 4
COL = 16 * DB
ROWS = K * NT
MESH = pl.DeviceIdType.MESH
AB = ((1,), (0,))
ABT = ((1,), (1,))
ATB = ((0,), (0,))
ORDER = [(ds, dc) for ds in (2, 1, 3, 0) for dc in (0, 1)]
PEERS = [p for p in ORDER if p != (0, 0)]
A, B = 0, 1
LAG = 3
ZLIST = sorted([(k + LAG * grp, grp, k) for grp in (A, B) for k in range(4)])


def dot(a, b, dims):
    return lax.dot_general(a, b, (dims, ((), ())), preferred_element_type=jnp.float32)


def place(t):
    return (t // 3) * 2 + t % 3 if t % 3 < 2 else 4 + t // 3


def al(v, n):
    return pl.multiple_of(v, n)


def kernel(owner_hbm, row_hbm, db_ref, gain_ref, wq_hbm, wo_hbm, q_hbm, k_hbm, v_hbm, t_hbm,
           att_hbm, gq_hbm, gk_hbm, gv_hbm,
           att_ref, gq_ref, gk_ref, gv_ref, who, row, req, rq, rqs, gath_a, gath_b, xs, xr, xm_a, xm_b, f_ref, wq_ref, wo_ref, q_ref, k_ref, v_ref, t_ref,
           normed, encq, probs, mixed, part_own, part_out, part_in, denc, denc_in, dmix,
           loc, rq_send, rq_recv, rx_send, rx_recv, sib_send, sib_recv, px_send, px_recv,
           zp_send, zp_recv, zm_send, zm_recv, x_send, x_recv, y_send, y_recv, m_send, m_recv,
           wy_send, wy_recv, ws_send, ws_recv, p_send, p_recv, d_send, d_recv, out_sem):
    s = lax.axis_index("section")
    d = lax.axis_index("shard")
    m = lax.axis_index("mp")
    x, z, c = d // 16, (d // 2) % 8, d % 2
    f32, bf = jnp.float32, jnp.bfloat16

    def dev(s_, x_, z_, c_, m_):
        return (s_, x_ * 16 + z_ * 2 + c_, m_)

    def peer(ds, dc):
        return dev((s + ds) % 4, x, z, (c + dc) % 2, m)

    pair = dev(s, 1 - x, z, c, m)
    up, down = dev(s, x, (z + 1) % 8, c, m), dev(s, x, (z + 7) % 8, c, m)
    mate = dev(s, x, z, c, 1 - m)
    sib = dev(s, x, z, 1 - c, m)
    me = s * 2 + c

    def remote(src, dst, ss, rs, to):
        return pltpu.make_async_remote_copy(src, dst, ss, rs, device_id=to, device_id_type=MESH)

    friends = [peer(*p) for p in PEERS] + [pair, up, down, mate]
    barrier = pltpu.get_barrier_semaphore()
    for f in friends:
        pl.semaphore_signal(barrier, inc=1, device_id=f, device_id_type=MESH)

    tok = pl.ds(al(s * TOK, TOK), TOK)

    def feat(core, ch):
        return pl.ds(al(((2 * m + core) * 3 + ch) * 128, 128), 128)

    def slot(ch, place):
        if ch < 2:
            return gath_a.at[pl.ds(place, DB), ch]
        return gath_b.at[x, pl.ds(place, DB)]

    here = z * 24 + c * DB
    small = [pltpu.make_async_copy(owner_hbm, who, loc.at[9]), pltpu.make_async_copy(row_hbm, row, loc.at[10])]
    for cp in small:
        cp.start()
    mine, to_sib = [], []
    for ch in range(3):
        cp = pltpu.make_async_copy(db_ref.at[:, tok, feat(c, ch)], slot(ch, here), loc.at[ch])
        cp.start()
        mine.append(cp)
    pl.semaphore_wait(barrier, len(friends))
    for ch in range(3):
        cp = remote(db_ref.at[:, tok, feat(1 - c, ch)], slot(ch, here), sib_send.at[ch], sib_recv.at[ch], sib)
        cp.start()
        to_sib.append(cp)
    to_pair = []
    for h in range(2):
        part = gath_b.at[x, pl.ds(z * 24 + ((c + h) % 2) * DB, DB)]
        to_pair.append(remote(part, part, px_send.at[h], px_recv.at[h], pair))
    lane = lax.broadcasted_iota(jnp.int32, (8, 128), 1)
    wanted = jnp.zeros((8, 128), jnp.int32)
    for cp in small:
        cp.wait()
    for j in range(REQ):
        g = who[j % K, j // K] * DB + row[j % K, j // K]
        wanted = jnp.where(lane == j, g, wanted)
    req[...] = wanted
    rq[x * 8 + me] = wanted
    rq_copies = []
    for i, p in enumerate(PEERS):
        cp = remote(req, rq.at[x * 8 + me], rq_send.at[i], rq_recv.at[i], peer(*p))
        cp.start()
        rq_copies.append(cp)

    plus, minus = {}, {}

    def zcopy(grp, k, h, up_way):
        zz = (z + 8 - k) % 8 if up_way else (z + k) % 8
        blocks = pl.ds(zz * 24 + ((c + h) % 2) * DB, DB)
        sl = gath_a.at[blocks] if grp == A else gath_b.at[:, blocks]
        i = grp * 7 + k * 2 + (h if k < 3 else 0)
        if up_way:
            return remote(sl, sl, zp_send.at[i], zp_recv.at[i], up)
        return remote(sl, sl, zm_send.at[i], zm_recv.at[i], down)

    def zstep(grp, k):
        for h in range(2):
            if k == 0:
                if grp == B:
                    to_pair[h].wait_recv()
                elif h == 0:
                    mine[0].wait()
                    mine[1].wait()
                else:
                    to_sib[0].wait_recv()
                    to_sib[1].wait_recv()
            ways = (True, False) if k < 3 else ((True,) if h == 0 else (False,))
            for way in ways:
                done = plus if way else minus
                if k:
                    done[grp, k - 1, h].wait_recv()
                cp = zcopy(grp, k, h, way)
                cp.start()
                done[grp, k, h] = cp

    def zdone(grp):
        plus[grp, 2, 1].wait_recv()
        minus[grp, 2, 0].wait_recv()
        plus[grp, 3, 0].wait_recv()
        minus[grp, 3, 1].wait_recv()

    def pair_out():
        mine[2].wait()
        to_pair[0].start()
        to_sib[2].wait_recv()
        to_pair[1].start()

    wy, ws, loads = [], [], []

    def weights_out():
        for w, (src, dst) in enumerate(((wq_hbm, wq_ref), (wo_hbm, wo_ref))):
            cp = pltpu.make_async_copy(src, dst.at[pl.ds(al(s * 384, 384), 384)], loc.at[3 + w])
            cp.start()
            loads.append(cp)
            for ds in (2, 1, 3):
                i = w * 3 + ds - 1
                cp = remote(src.at[pl.ds(al(c * 192, 192), 192)],
                            dst.at[pl.ds(al(s * 384 + c * 192, 192), 192)],
                            wy_send.at[i], wy_recv.at[i], peer(ds, 0))
                cp.start()
                wy.append((w, ds, cp))
        for i, (src, dst) in enumerate(((q_hbm, q_ref), (k_hbm, k_ref), (v_hbm, v_ref), (t_hbm, t_ref))):
            cp = pltpu.make_async_copy(src, dst, loc.at[5 + i])
            cp.start()
            loads.append(cp)

    def weights_on():
        for w, ds, cp in wy:
            cp.wait_recv()
            dst = (wq_ref, wo_ref)[w]
            part = dst.at[pl.ds(al(((s + 4 - ds) % 4) * 384 + c * 192, 192), 192)]
            i = w * 3 + ds - 1
            on = remote(part, part, ws_send.at[i], ws_recv.at[i], sib)
            on.start()
            ws.append(on)

    fwd = remote(rq.at[pl.ds(x * 8, 8)], rq.at[pl.ds(x * 8, 8)], rx_send.at[0], rx_recv.at[0], pair)

    def requests_on():
        for cp in rq_copies:
            cp.wait_recv()
        fwd.start()

    def requests_in():
        fwd.wait_recv()
        cp = pltpu.make_async_copy(rq, rqs, loc.at[11])
        cp.start()
        cp.wait()

    xcopies, ycopies, mcopies = {}, {}, []

    def target(i):
        ds, dc = ORDER[i]
        return ((s + ds) % 4) * 2 + (c + dc) % 2

    def select():
        for half in range(2):
            for i in range(half * 4, half * 4 + 4):
                for j in range(REQ):
                    g = rqs[(1 - x) * 8 + target(i), 0, j]
                    xs[i * 8 + j] = gath_a[lax.rem(g, COL)]
            part = pl.ds(half * 32, 32)
            cp = remote(xs.at[part], xr.at[part], x_send.at[half], x_recv.at[half], pair)
            cp.start()
            xcopies[half] = cp

    def deliver(grp, i):
        if grp == A:
            src, dst = xm_a.at[i], f_ref.at[pl.ds(m * 6 + c * 2, 2), :, pl.ds(al(s * 32, 32), 32), :]
        else:
            src, dst = xm_b.at[i], f_ref.at[m * 6 + 4 + c, :, pl.ds(al(s * 32, 32), 32), :]
        n = grp * 8 + i
        if ORDER[i] == (0, 0):
            cp = pltpu.make_async_copy(src, dst, y_recv.at[n])
        else:
            cp = remote(src, dst, y_send.at[n], y_recv.at[n], peer(*ORDER[i]))
        cp.start()
        ycopies[grp, i] = cp

    def merge_a(half):
        xcopies[half].wait_recv()
        for i in range(half * 4, half * 4 + 4):
            for j in range(REQ):
                g = rqs[x * 8 + target(i), 0, j]
                got = jnp.where((g // COL) == x, gath_a[lax.rem(g, COL)], xr[i * 8 + j])
                for ch in range(2):
                    xm_a[i, ch, j // K, (j % K) * TOK:(j % K + 1) * TOK] = got[ch]
            deliver(A, i)

    def merge_b():
        for i in range(8):
            for j in range(REQ):
                g = rqs[x * 8 + target(i), 0, j]
                xm_b[i, j // K, (j % K) * TOK:(j % K + 1) * TOK] = gath_b[g // COL, lax.rem(g, COL)]
            deliver(B, i)

    def arrived(grp, i):
        if ORDER[i] == (0, 0):
            ycopies[grp, i].wait()
        else:
            ycopies[grp, i].wait_recv()

    def onward(part, n):
        cp = remote(part, part, m_send.at[n], m_recv.at[n], mate)
        cp.start()
        mcopies.append(cp)

    def piece_a(i):
        ds, dc = ORDER[i]
        return f_ref.at[pl.ds(m * 6 + ((c + dc) % 2) * 2, 2), :, pl.ds(al(((s + 4 - ds) % 4) * 32, 32), 32), :]

    def piece_b(g):
        return f_ref.at[pl.ds(m * 6 + 4, 2), g]

    def onward_a(half):
        for i in range(half * 4, half * 4 + 4):
            arrived(A, i)
            onward(piece_a(i), i)

    def onward_b():
        for i in range(8):
            arrived(B, i)
        for g in range(SPANS):
            onward(piece_b(g), 8 + g)

    after = {
        (A, 0): [pair_out, weights_out],
        (A, 1): [requests_on],
        (A, 2): [requests_in],
        (B, 0): [lambda: zdone(A), select],
        (B, 2): [lambda: merge_a(0)],
        (B, 3): [lambda: merge_a(1), lambda: onward_a(0), lambda: onward_a(1), lambda: zdone(B), merge_b, weights_on,
                 onward_b],
    }
    for _, grp, k in ZLIST:
        zstep(grp, k)
        for act in after.get((grp, k), []):
            act()
    for i in range(8):
        remote(piece_a(i), piece_a(i), m_send.at[i], m_recv.at[i], mate).wait_recv()
    for cp in ws:
        cp.wait_recv()
    for cp in loads:
        cp.wait()

    scale = DH ** (-0.5)
    heads = q_ref.shape[1] // DH
    width = heads * DH
    own = pl.ds(al(m * width, 128), width)
    other = pl.ds(al((1 - m) * width, 128), width)

    def send(src, dst, ss, rs, g):
        rows = pl.ds(al(g * ROWS, ROWS), ROWS)
        return remote(src.at[rows], dst.at[rows], ss.at[g], rs.at[g], mate)

    outs = ((att_ref, att_hbm), (gq_ref, gq_hbm), (gk_ref, gk_hbm), (gv_ref, gv_hbm))

    def store(n, g):
        toks = pl.ds(al(g * CT, CT), CT)
        return pltpu.make_async_copy(outs[n][0].at[toks], outs[n][1].at[toks], out_sem.at[n, g])

    def encode(g, _):
        rows = pl.ds(al(g * ROWS, ROWS), ROWS)
        toks = pl.ds(al(g * CT, CT), CT)
        remote(piece_b(g), piece_b(g), m_send.at[8 + g], m_recv.at[8 + g], mate).wait_recv()
        squares = jnp.zeros((ROWS, 128), f32)
        for f in range(12):
            tile = f_ref[f, g].astype(f32)
            squares = squares + tile * tile
        mean = jnp.sum(squares, axis=1, keepdims=True) / (2 * width)
        inv = lax.rsqrt(mean + 1e-06)
        for t in range(12):
            f = (t // 6) * 6 + place(t % 6)
            gain = gain_ref[pl.ds(t * 128, 128)].reshape(1, 128)
            normed[:, t * 128:(t + 1) * 128] = (f_ref[f, g].astype(f32) * inv * gain).astype(bf)
        encq[rows, :] = dot(normed[...], wq_ref[...], AB).astype(bf)
        for h in range(heads):
            cols = slice(h * DH, (h + 1) * DH)
            st = dot(k_ref[toks, cols], encq[rows, cols], ABT) * scale
            e = jnp.exp(st - jnp.max(st, axis=0, keepdims=True))
            p = e / jnp.sum(e, axis=0, keepdims=True)
            probs[g * heads + h] = p
            mixed[:, cols] = dot(p.astype(bf), v_ref[toks, cols], ATB).astype(bf)
        part_out[rows, :] = dot(mixed[...], wo_ref[other, :], ABT).astype(bf)
        send(part_out, part_in, p_send, p_recv, g).start()
        part_own[rows, :] = dot(mixed[...], wo_ref[own, :], ABT)
        return 0

    def cross(g, _):
        rows = pl.ds(al(g * ROWS, ROWS), ROWS)
        toks = pl.ds(al(g * CT, CT), CT)
        send(part_out, part_in, p_send, p_recv, g).wait()
        for h in range(heads):
            cols = slice(h * DH, (h + 1) * DH)
            raw = f_ref[m * 6 + place(h), g].astype(f32)
            enc = (raw + (part_own[rows, cols] + part_in[rows, cols].astype(f32))).astype(bf)
            q, t = q_ref[toks, cols], t_ref[toks, cols]
            both = dot(jnp.concatenate([q, t], axis=0), enc, ABT)
            sc, dp = both[:CT] * scale, both[CT:]
            e = jnp.exp(sc - jnp.max(sc, axis=1, keepdims=True))
            p = e / jnp.sum(e, axis=1, keepdims=True)
            pb = p.astype(bf)
            dsc = (p * (dp - jnp.sum(dp * p, axis=1, keepdims=True))).astype(bf)
            out = dot(jnp.concatenate([pb, dsc], axis=0), enc, AB)
            att_ref[toks, cols] = out[:CT].astype(bf)
            gq_ref[toks, cols] = (scale * out[CT:]).astype(bf)
            denc[rows, cols] = (scale * dot(dsc, q, ATB) + dot(pb, t, ATB)).astype(bf)
        send(denc, denc_in, d_send, d_recv, g).start()
        store(0, g).start()
        store(1, g).start()
        return 0

    def back(g, _):
        rows = pl.ds(al(g * ROWS, ROWS), ROWS)
        toks = pl.ds(al(g * CT, CT), CT)
        near = dot(denc[rows, :], wo_ref[own, :], AB)
        send(denc, denc_in, d_send, d_recv, g).wait()
        dmix[...] = (near + dot(denc_in[rows, :], wo_ref[other, :], AB)).astype(bf)
        for h in range(heads):
            cols = slice(h * DH, (h + 1) * DH)
            p = probs[g * heads + h]
            dm = dmix[:, cols]
            gv_ref[toks, cols] = dot(p.astype(bf), dm, AB).astype(bf)
            dpe = dot(v_ref[toks, cols], dm, ABT)
            dse = (p * (dpe - jnp.sum(dpe * p, axis=0, keepdims=True))).astype(bf)
            gk_ref[toks, cols] = (scale * dot(dse, encq[rows, cols], AB)).astype(bf)
        store(2, g).start()
        store(3, g).start()
        return 0

    def both(g, _):
        encode(g, 0)
        return cross(g - 1, 0)

    encode(0, 0)
    lax.fori_loop(1, SPANS, both, 0)
    cross(SPANS - 1, 0)
    for cp in to_sib + to_pair + rq_copies + [fwd] + list(plus.values()) + list(minus.values()) + list(xcopies.values()):
        cp.wait_send()
    for (_, i), cp in ycopies.items():
        if ORDER[i] != (0, 0):
            cp.wait_send()
    for cp in mcopies + [cp for _, _, cp in wy] + ws:
        cp.wait_send()
    lax.fori_loop(0, SPANS, back, 0)
    for n in range(4):
        for g in range(SPANS):
            store(n, g).wait()


def hand_over(*refs):
    inward = [pltpu.make_async_copy(refs[i], refs[8].at[i], refs[9].at[i]) for i in range(4)]
    outward = [pltpu.make_async_copy(refs[8].at[i], refs[4 + i], refs[10].at[i]) for i in range(4)]
    for cp in inward:
        cp.start()
    for i in range(4):
        inward[i].wait()
        outward[i].start()
    for cp in outward:
        cp.wait()


def local(queries, ctx_keys, ctx_values, cotangent, owner, slot_row, database, enc_gain, enc_query_w, enc_out_w):
    dma = pltpu.SemaphoreType.DMA
    bf, f32, i32 = jnp.bfloat16, jnp.float32, jnp.int32
    tokens, half = queries.shape
    full = 2 * half
    rows = SPANS * ROWS
    heads = half // DH
    out = jax.ShapeDtypeStruct((tokens, half), bf)
    vmem, hbm = (pl.BlockSpec(memory_space=sp) for sp in (pltpu.VMEM, pltpu.HBM))
    results = pl.pallas_call(
        kernel,
        out_shape=(out,) * 4,
        in_specs=[hbm, hbm, hbm, vmem] + [hbm] * 6,
        out_specs=(hbm,) * 4,
        scratch_shapes=[
            pltpu.VMEM((tokens, half), bf),
            pltpu.VMEM((tokens, half), bf),
            pltpu.VMEM((tokens, half), bf),
            pltpu.VMEM((tokens, half), bf),
            pltpu.SMEM((K, SPANS), i32),
            pltpu.SMEM((K, SPANS), i32),
            pltpu.VMEM((8, 128), i32),
            pltpu.VMEM((16, 8, 128), i32),
            pltpu.SMEM((16, 8, 128), i32),
            pltpu.VMEM((COL, 2, TOK, 128), bf),
            pltpu.VMEM((2, COL, TOK, 128), bf),
            pltpu.VMEM((64, 2, TOK, 128), bf),
            pltpu.VMEM((64, 2, TOK, 128), bf),
            pltpu.VMEM((8, 2, SPANS, K * TOK, 128), bf),
            pltpu.VMEM((8, SPANS, K * TOK, 128), bf),
            pltpu.VMEM((12, SPANS, ROWS, 128), bf),
            pltpu.VMEM((full, half), bf),
            pltpu.VMEM((full, half), bf),
            pltpu.VMEM((tokens, half), bf),
            pltpu.VMEM((tokens, half), bf),
            pltpu.VMEM((tokens, half), bf),
            pltpu.VMEM((tokens, half), bf),
            pltpu.VMEM((ROWS, full), bf),
            pltpu.VMEM((rows, half), bf),
            pltpu.VMEM((SPANS * heads, CT, ROWS), f32),
            pltpu.VMEM((ROWS, half), bf),
            pltpu.VMEM((rows, half), f32),
            pltpu.VMEM((rows, half), bf),
            pltpu.VMEM((rows, half), bf),
            pltpu.VMEM((rows, half), bf),
            pltpu.VMEM((rows, half), bf),
            pltpu.VMEM((ROWS, half), bf),
            dma((12,)), dma((7,)), dma((7,)), dma((1,)), dma((1,)), dma((3,)), dma((3,)), dma((2,)), dma((2,)),
            dma((14,)), dma((14,)), dma((14,)), dma((14,)),
            dma((2,)), dma((2,)), dma((16,)), dma((16,)), dma((12,)), dma((12,)),
            dma((6,)), dma((6,)), dma((6,)), dma((6,)),
            dma((SPANS,)), dma((SPANS,)), dma((SPANS,)), dma((SPANS,)), dma((4, SPANS)),
        ],
        compiler_params=pltpu.CompilerParams(
            collective_id=0, has_side_effects=True, vmem_limit_bytes=63 * 1024 * 1024),
        cost_estimate=pl.CostEstimate(flops=4_600_000_000, bytes_accessed=12_000_000, transcendentals=600_000),
    )(owner.T, slot_row.T, database, enc_gain, enc_query_w, enc_out_w, queries, ctx_keys, ctx_values, cotangent)
    return pl.pallas_call(
        hand_over,
        out_shape=(out,) * 4,
        in_specs=[hbm] * 4,
        out_specs=(hbm,) * 4,
        scratch_shapes=[pltpu.VMEM((4, tokens, half), bf), dma((4,)), dma((4,))],
        cost_estimate=pl.CostEstimate(flops=0, bytes_accessed=4 * tokens * full, transcendentals=0),
    )(*results)


def solution(mesh):
    tokens = P(("section", "shard"), "mp")
    spans = P(("section", "shard"), None)
    weights = P("section", "mp")
    return jax.shard_map(
        local,
        mesh=mesh,
        in_specs=(tokens,) * 4 + (spans, spans, P("shard", None, None), P(), weights, weights),
        out_specs=(tokens,) * 4,
        check_vma=False,
    )
```

```python
import jax
import jax.numpy as jnp
from jax import lax
from jax.experimental import pallas as pl
from jax.experimental.pallas import tpu as pltpu
from jax.sharding import PartitionSpec as P

DH = 128
CT = 64
NT = 64
K = 2
DB = 12
SPANS = 4
REQ = SPANS * K
TOK = NT // 4
COL = 16 * DB
ROWS = K * NT
MESH = pl.DeviceIdType.MESH
AB = ((1,), (0,))
ABT = ((1,), (1,))
ATB = ((0,), (0,))
ORDER = [(ds, dx) for ds in (2, 1, 3, 0) for dx in (1, 0)]
PEERS = [p for p in ORDER if p != (0, 0)]

def dot(a, b, dims):
    return lax.dot_general(a, b, (dims, ((), ())), preferred_element_type=jnp.float32)


def place(t):
    return (t % 3) * 2 + t // 3


def al(v, n):
    return pl.multiple_of(v, n)


def kernel(owner_hbm, row_hbm, db_ref, gain_ref, wq_hbm, wo_hbm, q_hbm, k_hbm, v_hbm, t_hbm,
           att_hbm, gq_hbm, gk_hbm, gv_hbm,
           att_ref, gq_ref, gk_ref, gv_ref, who, row, req, rq, rqs, gath_0, gath_1, gath_2, xm, f_ref, wq_ref, wo_ref, q_ref, k_ref, v_ref, t_ref,
           normed, encq, probs, mixed, part_own, part_out, part_in, denc, denc_in, dmix,
           loc, rq_send, rq_recv, sib_send, sib_recv, px_send, px_recv,
           zp_send, zp_recv, zm_send, zm_recv, f_send, f_recv,
           wy_send, wy_recv, ws_send, ws_recv, p_send, p_recv, d_send, d_recv, out_sem):
    s = lax.axis_index("section")
    d = lax.axis_index("shard")
    m = lax.axis_index("mp")
    x, z, c = d // 16, (d // 2) % 8, d % 2
    f32, bf = jnp.float32, jnp.bfloat16
    gath = (gath_0, gath_1, gath_2)

    def dev(s_, x_, z_, c_, m_):
        return (s_, x_ * 16 + z_ * 2 + c_, m_)

    def peer(ds, dx, dm=0):
        return dev((s + ds) % 4, (x + dx) % 2, z, c, (m + dm) % 2)

    pair = peer(0, 1)
    up, down = dev(s, x, (z + 1) % 8, c, m), dev(s, x, (z + 7) % 8, c, m)
    mate = dev(s, x, z, c, 1 - m)
    sib = dev(s, x, z, 1 - c, m)
    me = s * 2 + x

    def remote(src, dst, ss, rs, to):
        return pltpu.make_async_remote_copy(src, dst, ss, rs, device_id=to, device_id_type=MESH)

    friends = [peer(*p) for p in PEERS] + [peer(*p, 1) for p in ORDER] + [sib, up, down]
    barrier = pltpu.get_barrier_semaphore()
    for f in friends:
        pl.semaphore_signal(barrier, inc=1, device_id=f, device_id_type=MESH)

    tok = pl.ds(al(s * TOK, TOK), TOK)

    def feat(column, ch):
        return pl.ds(al(((2 * m + column) * 3 + ch) * 128, 128), 128)

    def blocks(zz):
        return pl.ds(zz * 24 + c * DB, DB)

    small = [pltpu.make_async_copy(owner_hbm, who, loc.at[9]), pltpu.make_async_copy(row_hbm, row, loc.at[10])]
    for cp in small:
        cp.start()
    mine, to_pair = [], []
    for ch in range(3):
        cp = pltpu.make_async_copy(db_ref.at[:, tok, feat(x, ch)], gath[ch].at[x, blocks(z)], loc.at[ch])
        cp.start()
        mine.append(cp)
    pl.semaphore_wait(barrier, len(friends))
    for ch in range(3):
        cp = remote(db_ref.at[:, tok, feat(1 - x, ch)], gath[ch].at[x, blocks(z)], px_send.at[ch], px_recv.at[ch], pair)
        cp.start()
        to_pair.append(cp)
    lane = lax.broadcasted_iota(jnp.int32, (8, 128), 1)
    wanted = jnp.zeros((8, 128), jnp.int32)
    for cp in small:
        cp.wait()
    for j in range(REQ):
        g = who[j % K, j // K] * DB + row[j % K, j // K]
        wanted = jnp.where(lane == j, g, wanted)
    req[...] = wanted
    rq[me] = wanted
    rq_copies = []
    for i, p in enumerate(PEERS):
        cp = remote(req, rq.at[me], rq_send.at[i], rq_recv.at[i], peer(*p))
        cp.start()
        rq_copies.append(cp)

    plus, minus, shares = {}, {}, {}

    def zcopy(ch, k, h, up_way):
        zz = (z + 8 - k) % 8 if up_way else (z + k) % 8
        sl = gath[ch].at[(x + h) % 2, blocks(zz)]
        i = ch * 7 + k * 2 + (h if k < 3 else 0)
        if up_way:
            return remote(sl, sl, zp_send.at[i], zp_recv.at[i], up)
        return remote(sl, sl, zm_send.at[i], zm_recv.at[i], down)

    def share(ch, n, zz):
        sl = gath[ch].at[:, blocks(zz)]
        shares[ch, n] = remote(sl, sl, sib_send.at[ch * 8 + n], sib_recv.at[ch * 8 + n], sib)
        shares[ch, n].start()

    def zstep(ch, k, h):
        if k:
            plus[ch, k - 1, h].wait_recv()
            minus[ch, k - 1, h].wait_recv()
        elif h == 0:
            mine[ch].wait()
        else:
            to_pair[ch].wait_recv()
        for way in (True, False):
            if k < 3 or way == (h == 0):
                cp = zcopy(ch, k, h, way)
                cp.start()
                (plus if way else minus)[ch, k, h] = cp
        if h and k:
            share(ch, 2 * k - 1, (z + 8 - k) % 8)
            share(ch, 2 * k, (z + k) % 8)
        elif h:
            share(ch, 0, z)

    def zdone(ch):
        plus[ch, 3, 0].wait_recv()
        minus[ch, 3, 1].wait_recv()
        share(ch, 7, (z + 4) % 8)
        for n in range(8):
            shares[ch, n].wait_recv()

    loads, wy, ws = {}, {}, {}
    wsrc, wdst = (wq_hbm, wo_hbm), (wq_ref, wo_ref)

    def spans_in():
        for i, (src, dst) in enumerate(((q_hbm, q_ref), (k_hbm, k_ref), (v_hbm, v_ref), (t_hbm, t_ref))):
            loads["qkvt"[i]] = pltpu.make_async_copy(src, dst, loc.at[5 + i])
            loads["qkvt"[i]].start()

    def wcopy(w, ds, sec, to):
        part = wdst[w].at[pl.ds(al(sec * 384 + c * 192, 192), 192)]
        src = wsrc[w].at[pl.ds(al(c * 192, 192), 192)] if ds != 2 else part
        i = w * 3 + ds - 1
        return remote(src, part, wy_send.at[i], wy_recv.at[i], peer(to, 0))

    def weights_out(w):
        loads[w] = pltpu.make_async_copy(wsrc[w], wdst[w].at[pl.ds(al(s * 384, 384), 384)], loc.at[3 + w])
        loads[w].start()
        for ds in (1, 3):
            wy[w, ds] = wcopy(w, ds, s, ds)
            wy[w, ds].start()

    def weights_relay():
        for w, ds in ((0, 1), (1, 3)):
            wy[w, ds].wait_recv()
            wy[w, 2] = wcopy(w, 2, (s + 4 - ds) % 4, ds)
            wy[w, 2].start()

    def weights_on(w):
        for ds in (1, 3, 2):
            if (w, ds) not in ((0, 1), (1, 3)):
                wy[w, ds].wait_recv()
            part = wdst[w].at[pl.ds(al(((s + 4 - ds) % 4) * 384 + c * 192, 192), 192)]
            i = w * 3 + ds - 1
            ws[w, ds] = remote(part, part, ws_send.at[i], ws_recv.at[i], sib)
            ws[w, ds].start()

    def weights_here(w):
        loads[w].wait()
        for ds in (1, 3, 2):
            ws[w, ds].wait_recv()

    def requests_in():
        for cp in rq_copies:
            cp.wait_recv()
        cp = pltpu.make_async_copy(rq, rqs, loc.at[11])
        cp.start()
        cp.wait()

    fcopies = {}

    def deliver(ch):
        for i, (ds, dx) in enumerate(ORDER):
            for j in range(REQ):
                g = rqs[((s + ds) % 4) * 2 + (x + dx) % 2, 0, j]
                xm[ch, i, j // K, (j % K) * TOK:(j % K + 1) * TOK] = gath[ch][g // COL, lax.rem(g, COL)]
            src, dst = xm.at[ch, i], f_ref.at[m * 6 + ch * 2 + x, :, pl.ds(al(s * 32, 32), 32), :]
            for dm in (1, 0):
                n = (ch * 8 + i) * 2 + dm
                if (ds, dx, dm) == (0, 0, 0):
                    cp = pltpu.make_async_copy(src, dst, f_recv.at[n])
                else:
                    cp = remote(src, dst, f_send.at[n], f_recv.at[n], peer(ds, dx, dm))
                cp.start()
                fcopies[n] = cp

    def arrived():
        for n, cp in fcopies.items():
            if n % 16 == 14:
                cp.wait()
            else:
                cp.wait_recv()

    for ch in (0, 2, 1):
        zstep(ch, 0, 0)
    weights_out(0)
    weights_out(1)
    zstep(0, 0, 1)
    zstep(0, 1, 0)
    zstep(1, 1, 0)
    zstep(0, 1, 1)
    zstep(0, 2, 0)
    zstep(1, 0, 1)
    zstep(0, 2, 1)
    zstep(2, 0, 1)
    zstep(1, 1, 1)
    requests_in()
    spans_in()
    zstep(0, 3, 0)
    zstep(0, 3, 1)
    zstep(1, 2, 0)
    zstep(1, 2, 1)
    weights_relay()
    zstep(2, 1, 0)
    zstep(2, 1, 1)
    zdone(0)
    deliver(0)
    zstep(1, 3, 0)
    zstep(1, 3, 1)
    zstep(2, 2, 0)
    zstep(2, 2, 1)
    zdone(1)
    deliver(1)
    zstep(2, 3, 0)
    zstep(2, 3, 1)
    zdone(2)
    deliver(2)
    weights_on(0)
    weights_on(1)
    arrived()
    weights_here(0)
    for name in "qkvt":
        loads[name].wait()
    weights_here(1)

    scale = DH ** (-0.5)
    heads = q_ref.shape[1] // DH
    width = heads * DH
    own = pl.ds(al(m * width, 128), width)
    other = pl.ds(al((1 - m) * width, 128), width)

    def send(src, dst, ss, rs, g):
        rows = pl.ds(al(g * ROWS, ROWS), ROWS)
        return remote(src.at[rows], dst.at[rows], ss.at[g], rs.at[g], mate)

    outs = ((att_ref, att_hbm), (gq_ref, gq_hbm), (gk_ref, gk_hbm), (gv_ref, gv_hbm))

    def store(n, g):
        toks = pl.ds(al(g * CT, CT), CT)
        return pltpu.make_async_copy(outs[n][0].at[toks], outs[n][1].at[toks], out_sem.at[n, g])

    def encode(g, _):
        rows = pl.ds(al(g * ROWS, ROWS), ROWS)
        toks = pl.ds(al(g * CT, CT), CT)
        squares = jnp.zeros((ROWS, 128), f32)
        for f in range(12):
            tile = f_ref[f, g].astype(f32)
            squares = squares + tile * tile
        mean = jnp.sum(squares, axis=1, keepdims=True) / (2 * width)
        inv = lax.rsqrt(mean + 1e-06)
        for t in range(12):
            f = (t // 6) * 6 + place(t % 6)
            gain = gain_ref[pl.ds(t * 128, 128)].reshape(1, 128)
            normed[:, t * 128:(t + 1) * 128] = (f_ref[f, g].astype(f32) * inv * gain).astype(bf)
        encq[rows, :] = dot(normed[...], wq_ref[...], AB).astype(bf)
        for h in range(heads):
            cols = slice(h * DH, (h + 1) * DH)
            st = dot(k_ref[toks, cols], encq[rows, cols], ABT) * scale
            e = jnp.exp(st - jnp.max(st, axis=0, keepdims=True))
            p = e / jnp.sum(e, axis=0, keepdims=True)
            probs[g * heads + h] = p
            mixed[:, cols] = dot(p.astype(bf), v_ref[toks, cols], ATB).astype(bf)
        part_out[rows, :] = dot(mixed[...], wo_ref[other, :], ABT).astype(bf)
        send(part_out, part_in, p_send, p_recv, g).start()
        part_own[rows, :] = dot(mixed[...], wo_ref[own, :], ABT)
        return 0

    def cross(g, _):
        rows = pl.ds(al(g * ROWS, ROWS), ROWS)
        toks = pl.ds(al(g * CT, CT), CT)
        send(part_out, part_in, p_send, p_recv, g).wait()
        for h in range(heads):
            cols = slice(h * DH, (h + 1) * DH)
            raw = f_ref[m * 6 + place(h), g].astype(f32)
            enc = (raw + (part_own[rows, cols] + part_in[rows, cols].astype(f32))).astype(bf)
            qt = jnp.concatenate([q_ref[toks, cols], t_ref[toks, cols]], axis=0)
            both = dot(qt, enc, ABT)
            sc, dp = both[:CT] * scale, both[CT:]
            e = jnp.exp(sc - jnp.max(sc, axis=1, keepdims=True))
            p = e / jnp.sum(e, axis=1, keepdims=True)
            dsc = scale * (p * (dp - jnp.sum(dp * p, axis=1, keepdims=True)))
            dsp = jnp.concatenate([dsc.astype(bf), p.astype(bf)], axis=0)
            out = dot(dsp, enc, AB).astype(bf)
            gq_ref[toks, cols] = out[:CT]
            att_ref[toks, cols] = out[CT:]
            denc[rows, cols] = dot(dsp, qt, ATB).astype(bf)
        send(denc, denc_in, d_send, d_recv, g).start()
        store(0, g).start()
        store(1, g).start()
        return 0

    def back(g, _):
        rows = pl.ds(al(g * ROWS, ROWS), ROWS)
        toks = pl.ds(al(g * CT, CT), CT)
        near = dot(denc[rows, :], wo_ref[own, :], AB)
        send(denc, denc_in, d_send, d_recv, g).wait()
        dmix[...] = (near + dot(denc_in[rows, :], wo_ref[other, :], AB)).astype(bf)
        for h in range(heads):
            cols = slice(h * DH, (h + 1) * DH)
            p = probs[g * heads + h]
            dm = dmix[:, cols]
            gv_ref[toks, cols] = dot(p.astype(bf), dm, AB).astype(bf)
            dpe = dot(v_ref[toks, cols], dm, ABT)
            dse = (p * (dpe - jnp.sum(dpe * p, axis=0, keepdims=True))).astype(bf)
            gk_ref[toks, cols] = (scale * dot(dse, encq[rows, cols], AB)).astype(bf)
        store(2, g).start()
        store(3, g).start()
        return 0

    def both(g, _):
        encode(g, 0)
        return cross(g - 1, 0)

    encode(0, 0)
    lax.fori_loop(1, SPANS, both, 0)
    cross(SPANS - 1, 0)
    for cp in to_pair + rq_copies + list(plus.values()) + list(minus.values()) + list(shares.values()):
        cp.wait_send()
    for n, cp in fcopies.items():
        if n % 16 != 14:
            cp.wait_send()
    for cp in list(wy.values()) + list(ws.values()):
        cp.wait_send()
    lax.fori_loop(0, SPANS, back, 0)
    for n in range(4):
        for g in range(SPANS):
            store(n, g).wait()


def hand_over(*refs):
    inward = [pltpu.make_async_copy(refs[i], refs[8].at[i], refs[9].at[i]) for i in range(4)]
    outward = [pltpu.make_async_copy(refs[8].at[i], refs[4 + i], refs[10].at[i]) for i in range(4)]
    for cp in inward:
        cp.start()
    for i in range(4):
        inward[i].wait()
        outward[i].start()
    for cp in outward:
        cp.wait()


def local(queries, ctx_keys, ctx_values, cotangent, owner, slot_row, database, enc_gain, enc_query_w, enc_out_w):
    dma = pltpu.SemaphoreType.DMA
    bf, f32, i32 = jnp.bfloat16, jnp.float32, jnp.int32
    tokens, half = queries.shape
    full = 2 * half
    rows = SPANS * ROWS
    heads = half // DH
    out = jax.ShapeDtypeStruct((tokens, half), bf)
    vmem, hbm = (pl.BlockSpec(memory_space=sp) for sp in (pltpu.VMEM, pltpu.HBM))
    results = pl.pallas_call(
        kernel,
        out_shape=(out,) * 4,
        in_specs=[hbm, hbm, hbm, vmem] + [hbm] * 6,
        out_specs=(hbm,) * 4,
        scratch_shapes=[
            pltpu.VMEM((tokens, half), bf),
            pltpu.VMEM((tokens, half), bf),
            pltpu.VMEM((tokens, half), bf),
            pltpu.VMEM((tokens, half), bf),
            pltpu.SMEM((K, SPANS), i32),
            pltpu.SMEM((K, SPANS), i32),
            pltpu.VMEM((8, 128), i32),
            pltpu.VMEM((8, 8, 128), i32),
            pltpu.SMEM((8, 8, 128), i32),
            pltpu.VMEM((2, COL, TOK, 128), bf),
            pltpu.VMEM((2, COL, TOK, 128), bf),
            pltpu.VMEM((2, COL, TOK, 128), bf),
            pltpu.VMEM((3, 8, SPANS, K * TOK, 128), bf),
            pltpu.VMEM((12, SPANS, ROWS, 128), bf),
            pltpu.VMEM((full, half), bf),
            pltpu.VMEM((full, half), bf),
            pltpu.VMEM((tokens, half), bf),
            pltpu.VMEM((tokens, half), bf),
            pltpu.VMEM((tokens, half), bf),
            pltpu.VMEM((tokens, half), bf),
            pltpu.VMEM((ROWS, full), bf),
            pltpu.VMEM((rows, half), bf),
            pltpu.VMEM((SPANS * heads, CT, ROWS), f32),
            pltpu.VMEM((ROWS, half), bf),
            pltpu.VMEM((rows, half), f32),
            pltpu.VMEM((rows, half), bf),
            pltpu.VMEM((rows, half), bf),
            pltpu.VMEM((rows, half), bf),
            pltpu.VMEM((rows, half), bf),
            pltpu.VMEM((ROWS, half), bf),
            dma((12,)), dma((7,)), dma((7,)), dma((24,)), dma((24,)), dma((3,)), dma((3,)),
            dma((21,)), dma((21,)), dma((21,)), dma((21,)), dma((48,)), dma((48,)),
            dma((6,)), dma((6,)), dma((6,)), dma((6,)),
            dma((SPANS,)), dma((SPANS,)), dma((SPANS,)), dma((SPANS,)), dma((4, SPANS)),
        ],
        compiler_params=pltpu.CompilerParams(
            collective_id=0, has_side_effects=True, vmem_limit_bytes=63 * 1024 * 1024),
        cost_estimate=pl.CostEstimate(flops=4_600_000_000, bytes_accessed=12_000_000, transcendentals=600_000),
    )(owner.T, slot_row.T, database, enc_gain, enc_query_w, enc_out_w, queries, ctx_keys, ctx_values, cotangent)
    return pl.pallas_call(
        hand_over,
        out_shape=(out,) * 4,
        in_specs=[hbm] * 4,
        out_specs=(hbm,) * 4,
        scratch_shapes=[pltpu.VMEM((4, tokens, half), bf), dma((4,)), dma((4,))],
        cost_estimate=pl.CostEstimate(flops=0, bytes_accessed=4 * tokens * full, transcendentals=0),
    )(*results)


def solution(mesh):
    tokens = P(("section", "shard"), "mp")
    spans = P(("section", "shard"), None)
    weights = P("section", "mp")
    return jax.shard_map(
        local,
        mesh=mesh,
        in_specs=(tokens,) * 4 + (spans, spans, P("shard", None, None), P(), weights, weights),
        out_specs=(tokens,) * 4,
        check_vma=False,
    )
```

```python
import jax
import jax.numpy as jnp
from jax import lax
from jax.experimental import pallas as pl
from jax.experimental.pallas import tpu as pltpu
from jax.sharding import PartitionSpec as P

DH = 128
CT = 64
NT = 64
K = 2
DB = 12
SPANS = 4
REQ = SPANS * K
TOK = NT // 4
COL = 16 * DB
ROWS = K * NT
MESH = pl.DeviceIdType.MESH
AB = ((1,), (0,))
ABT = ((1,), (1,))
ATB = ((0,), (0,))
ORDER = [(ds, dx) for ds in (2, 1, 3, 0) for dx in (1, 0)]
PEERS = [p for p in ORDER if p != (0, 0)]

def dot(a, b, dims):
    return lax.dot_general(a, b, (dims, ((), ())), preferred_element_type=jnp.float32)


def place(t):
    return (t % 3) * 2 + t // 3


def al(v, n):
    return pl.multiple_of(v, n)


def kernel(owner_hbm, row_hbm, db_ref, gain_ref, wq_hbm, wo_hbm, q_hbm, k_hbm, v_hbm, t_hbm,
           att_hbm, gq_hbm, gk_hbm, gv_hbm,
           att_ref, gq_ref, gk_ref, gv_ref, who, row, req, rq, rqs, gath_0, gath_1, gath_2, xm, f_ref, wq_ref, wo_ref, q_ref, k_ref, v_ref, t_ref,
           normed, encq, probs, pb_out, pb_in, v2_ref, w2_ref, mixed, part_own, denc, denc_in, dmix,
           loc, rq_send, rq_recv, sib_send, sib_recv, px_send, px_recv,
           zp_send, zp_recv, zm_send, zm_recv, f_send, f_recv,
           wy_send, wy_recv, ws_send, ws_recv, v_send, v_recv, w2_send, w2_recv, w2s_send, w2s_recv, p_send, p_recv, d_send, d_recv, out_sem):
    s = lax.axis_index("section")
    d = lax.axis_index("shard")
    m = lax.axis_index("mp")
    x, z, c = d // 16, (d // 2) % 8, d % 2
    f32, bf = jnp.float32, jnp.bfloat16
    gath = (gath_0, gath_1, gath_2)

    def dev(s_, x_, z_, c_, m_):
        return (s_, x_ * 16 + z_ * 2 + c_, m_)

    def peer(ds, dx, dm=0):
        return dev((s + ds) % 4, (x + dx) % 2, z, c, (m + dm) % 2)

    pair = peer(0, 1)
    up, down = dev(s, x, (z + 1) % 8, c, m), dev(s, x, (z + 7) % 8, c, m)
    mate = dev(s, x, z, c, 1 - m)
    sib = dev(s, x, z, 1 - c, m)
    me = s * 2 + x

    def remote(src, dst, ss, rs, to):
        return pltpu.make_async_remote_copy(src, dst, ss, rs, device_id=to, device_id_type=MESH)

    friends = [peer(*p) for p in PEERS] + [peer(*p, 1) for p in ORDER] + [sib, up, down]
    barrier = pltpu.get_barrier_semaphore()
    for f in friends:
        pl.semaphore_signal(barrier, inc=1, device_id=f, device_id_type=MESH)

    tok = pl.ds(al(s * TOK, TOK), TOK)

    def feat(column, ch):
        return pl.ds(al(((2 * m + column) * 3 + ch) * 128, 128), 128)

    def blocks(zz):
        return pl.ds(zz * 24 + c * DB, DB)

    small = [pltpu.make_async_copy(owner_hbm, who, loc.at[9]), pltpu.make_async_copy(row_hbm, row, loc.at[10])]
    for cp in small:
        cp.start()
    mine, to_pair = [], []
    for ch in range(3):
        cp = pltpu.make_async_copy(db_ref.at[:, tok, feat(x, ch)], gath[ch].at[x, blocks(z)], loc.at[ch])
        cp.start()
        mine.append(cp)
    pl.semaphore_wait(barrier, len(friends))
    for ch in range(3):
        cp = remote(db_ref.at[:, tok, feat(1 - x, ch)], gath[ch].at[x, blocks(z)], px_send.at[ch], px_recv.at[ch], pair)
        cp.start()
        to_pair.append(cp)
    lane = lax.broadcasted_iota(jnp.int32, (8, 128), 1)
    wanted = jnp.zeros((8, 128), jnp.int32)
    for cp in small:
        cp.wait()
    for j in range(REQ):
        g = who[j % K, j // K] * DB + row[j % K, j // K]
        wanted = jnp.where(lane == j, g, wanted)
    req[...] = wanted
    rq[me] = wanted
    rq_copies = []
    for i, p in enumerate(PEERS):
        cp = remote(req, rq.at[me], rq_send.at[i], rq_recv.at[i], peer(*p))
        cp.start()
        rq_copies.append(cp)

    plus, minus, shares = {}, {}, {}

    def zcopy(ch, k, h, up_way):
        zz = (z + 8 - k) % 8 if up_way else (z + k) % 8
        sl = gath[ch].at[(x + h) % 2, blocks(zz)]
        i = ch * 7 + k * 2 + (h if k < 3 else 0)
        if up_way:
            return remote(sl, sl, zp_send.at[i], zp_recv.at[i], up)
        return remote(sl, sl, zm_send.at[i], zm_recv.at[i], down)

    def share(ch, n, zz):
        sl = gath[ch].at[:, blocks(zz)]
        shares[ch, n] = remote(sl, sl, sib_send.at[ch * 8 + n], sib_recv.at[ch * 8 + n], sib)
        shares[ch, n].start()

    def zstep(ch, k, h):
        if k:
            plus[ch, k - 1, h].wait_recv()
            minus[ch, k - 1, h].wait_recv()
        elif h == 0:
            mine[ch].wait()
        else:
            to_pair[ch].wait_recv()
        for way in (True, False):
            if k < 3 or way == (h == 0):
                cp = zcopy(ch, k, h, way)
                cp.start()
                (plus if way else minus)[ch, k, h] = cp
        if h and k:
            share(ch, 2 * k - 1, (z + 8 - k) % 8)
            share(ch, 2 * k, (z + k) % 8)
        elif h:
            share(ch, 0, z)

    def zdone(ch):
        plus[ch, 3, 0].wait_recv()
        minus[ch, 3, 1].wait_recv()
        share(ch, 7, (z + 4) % 8)
        for n in range(8):
            shares[ch, n].wait_recv()

    loads, wy, ws = {}, {}, {}
    wsrc, wdst = (wq_hbm, wo_hbm), (wq_ref, wo_ref)

    def spans_in():
        for i, (src, dst) in enumerate(((q_hbm, q_ref), (k_hbm, k_ref), (v_hbm, v_ref), (t_hbm, t_ref))):
            loads["qkvt"[i]] = pltpu.make_async_copy(src, dst, loc.at[5 + i])
            loads["qkvt"[i]].start()

    def wcopy(w, ds, sec, to):
        part = wdst[w].at[pl.ds(al(sec * 384 + c * 192, 192), 192)]
        src = wsrc[w].at[pl.ds(al(c * 192, 192), 192)] if ds != 2 else part
        i = w * 3 + ds - 1
        return remote(src, part, wy_send.at[i], wy_recv.at[i], peer(to, 0))

    def weights_out(w):
        loads[w] = pltpu.make_async_copy(wsrc[w], wdst[w].at[pl.ds(al(s * 384, 384), 384)], loc.at[3 + w])
        loads[w].start()
        for ds in (1, 3):
            wy[w, ds] = wcopy(w, ds, s, ds)
            wy[w, ds].start()

    def weights_relay():
        for w, ds in ((0, 1), (1, 3)):
            wy[w, ds].wait_recv()
            wy[w, 2] = wcopy(w, 2, (s + 4 - ds) % 4, ds)
            wy[w, 2].start()

    def weights_on(w):
        for ds in (1, 3, 2):
            if (w, ds) not in ((0, 1), (1, 3)):
                wy[w, ds].wait_recv()
            part = wdst[w].at[pl.ds(al(((s + 4 - ds) % 4) * 384 + c * 192, 192), 192)]
            i = w * 3 + ds - 1
            ws[w, ds] = remote(part, part, ws_send.at[i], ws_recv.at[i], sib)
            ws[w, ds].start()

    def weights_here(w):
        loads[w].wait()
        for ds in (1, 3, 2):
            ws[w, ds].wait_recv()

    v_out = remote(v_hbm, v2_ref, v_send.at[0], v_recv.at[0], mate)

    def w2_rows(u):
        return w2_ref.at[pl.ds(al(u * 384 + c * 192, 192), 192)]

    role = (s + 4 - 2 * m) % 4
    first = ((role + 1) // 2) % 2

    def w2_first():
        return remote(wo_hbm.at[pl.ds(al(c * 192, 192), 192)], w2_rows(s % 2), w2_send.at[0], w2_recv.at[s % 2], mate)

    def w2_next(ds):
        return remote(w2_rows(first), w2_rows(first), w2_send.at[ds], w2_recv.at[first], peer(ds, 0))

    def w2_wait(u):
        remote(w2_rows(u), w2_rows(u), w2_send.at[0], w2_recv.at[u], mate).wait_recv()

    def w2_sib(u):
        return remote(w2_rows(u), w2_rows(u), w2s_send.at[u], w2s_recv.at[u], sib)

    def others_out():
        @pl.when(s // 2 == 1 - m)
        def _():
            w2_first().start()

    def w2_spread():
        @pl.when(role < 2)
        def _():
            w2_wait(first)
            w2_next(1).start()
            w2_next(3).start()

    def w2_relay():
        @pl.when(role == 2)
        def _():
            w2_wait(first)
            w2_next(1).start()

        @pl.when(role == 3)
        def _():
            w2_wait(first)
            w2_next(3).start()

    def w2_on():
        w2_sib(first).start()
        w2_wait(1 - first)
        w2_sib(1 - first).start()

    def w2_here():
        for u in range(2):
            w2_sib(u).wait_recv()

    def w2_sent():
        @pl.when(s // 2 == 1 - m)
        def _():
            w2_first().wait_send()

        @pl.when(role != 3)
        def _():
            w2_next(1).wait_send()

        @pl.when(role != 2)
        def _():
            w2_next(3).wait_send()

        for u in range(2):
            w2_sib(u).wait_send()

    def requests_in():
        for cp in rq_copies:
            cp.wait_recv()
        cp = pltpu.make_async_copy(rq, rqs, loc.at[11])
        cp.start()
        cp.wait()

    fcopies = {}

    def deliver(ch, spans=(0, SPANS), base=None):
        base = ch * 16 if base is None else base
        some = pl.ds(spans[0], spans[1] - spans[0])
        for i, (ds, dx) in enumerate(ORDER):
            for j in range(spans[0] * K, spans[1] * K):
                g = rqs[((s + ds) % 4) * 2 + (x + dx) % 2, 0, j]
                xm[ch, i, j // K, (j % K) * TOK:(j % K + 1) * TOK] = gath[ch][g // COL, lax.rem(g, COL)]
            src = xm.at[ch, i, some]
            dst = f_ref.at[m * 6 + ch * 2 + x, some, pl.ds(al(s * 32, 32), 32), :]
            for dm in (1, 0):
                n = base + i * 2 + dm
                if (ds, dx, dm) == (0, 0, 0):
                    cp = pltpu.make_async_copy(src, dst, f_recv.at[n])
                else:
                    cp = remote(src, dst, f_send.at[n], f_recv.at[n], peer(ds, dx, dm))
                cp.start()
                fcopies[n] = cp

    def arrived(first, last):
        for n in range(first, last):
            if n % 16 == 14:
                fcopies[n].wait()
            else:
                fcopies[n].wait_recv()

    for ch in (0, 2, 1):
        zstep(ch, 0, 0)
    weights_out(0)
    others_out()
    weights_out(1)
    zstep(0, 0, 1)
    zstep(0, 1, 0)
    zstep(1, 1, 0)
    zstep(0, 1, 1)
    zstep(0, 2, 0)
    zstep(1, 0, 1)
    zstep(0, 2, 1)
    zstep(2, 0, 1)
    zstep(1, 1, 1)
    requests_in()
    spans_in()
    v_out.start()
    zstep(0, 3, 0)
    zstep(0, 3, 1)
    zstep(1, 2, 0)
    zstep(1, 2, 1)
    w2_spread()
    weights_relay()
    zstep(2, 1, 0)
    zstep(2, 1, 1)
    zdone(0)
    deliver(0)
    zstep(1, 3, 0)
    zstep(1, 3, 1)
    zstep(2, 2, 0)
    zstep(2, 2, 1)
    zdone(1)
    deliver(1)
    zstep(2, 3, 0)
    zstep(2, 3, 1)
    zdone(2)
    deliver(2, (0, 2), 32)
    deliver(2, (2, 4), 48)
    w2_relay()
    weights_on(0)
    arrived(0, 48)
    weights_here(0)
    for name in "qkvt":
        loads[name].wait()

    scale = DH ** (-0.5)
    heads = q_ref.shape[1] // DH
    width = heads * DH
    own = pl.ds(al(m * width, 128), width)
    other = pl.ds(al((1 - m) * width, 128), width)

    def send(src, dst, ss, rs, g):
        rows = pl.ds(al(g * ROWS, ROWS), ROWS)
        return remote(src.at[rows], dst.at[rows], ss.at[g], rs.at[g], mate)

    outs = ((att_ref, att_hbm), (gq_ref, gq_hbm), (gk_ref, gk_hbm), (gv_ref, gv_hbm))

    def store(n, g):
        toks = pl.ds(al(g * CT, CT), CT)
        return pltpu.make_async_copy(outs[n][0].at[toks], outs[n][1].at[toks], out_sem.at[n, g])

    def send_p(g):
        part = pl.ds(g * heads, heads)
        return remote(pb_out.at[part], pb_in.at[part], p_send.at[g], p_recv.at[g], mate)

    def encode(g, _):
        rows = pl.ds(al(g * ROWS, ROWS), ROWS)
        toks = pl.ds(al(g * CT, CT), CT)
        squares = jnp.zeros((ROWS, 128), f32)
        for f in range(12):
            tile = f_ref[f, g].astype(f32)
            squares = squares + tile * tile
        mean = jnp.sum(squares, axis=1, keepdims=True) / (2 * width)
        inv = lax.rsqrt(mean + 1e-06)
        for t in range(12):
            f = (t // 6) * 6 + place(t % 6)
            gain = gain_ref[pl.ds(t * 128, 128)].reshape(1, 128)
            normed[:, t * 128:(t + 1) * 128] = (f_ref[f, g].astype(f32) * inv * gain).astype(bf)
        encq[rows, :] = dot(normed[...], wq_ref[...], AB).astype(bf)
        for h in range(heads):
            cols = slice(h * DH, (h + 1) * DH)
            st = dot(k_ref[toks, cols], encq[rows, cols], ABT) * scale
            e = jnp.exp(st - jnp.max(st, axis=0, keepdims=True))
            p = e / jnp.sum(e, axis=0, keepdims=True)
            probs[g * heads + h] = p
            pb_out[g * heads + h] = p.astype(bf)
        send_p(g).start()
        return 0

    def cross(g, _):
        rows = pl.ds(al(g * ROWS, ROWS), ROWS)
        toks = pl.ds(al(g * CT, CT), CT)
        for h in range(heads):
            cols = slice(h * DH, (h + 1) * DH)
            mixed[:, cols] = dot(pb_out[g * heads + h], v_ref[toks, cols], ATB).astype(bf)
        part_own[...] = dot(mixed[...], wo_ref[own, :], ABT)
        send_p(g).wait()
        for h in range(heads):
            cols = slice(h * DH, (h + 1) * DH)
            mixed[:, cols] = dot(pb_in[g * heads + h], v2_ref[toks, cols], ATB).astype(bf)
        part_own[...] += dot(mixed[...], w2_ref[...], ABT)
        for h in range(heads):
            cols = slice(h * DH, (h + 1) * DH)
            raw = f_ref[m * 6 + place(h), g].astype(f32)
            enc = (raw + part_own[:, cols]).astype(bf)
            qt = jnp.concatenate([q_ref[toks, cols], t_ref[toks, cols]], axis=0)
            both = dot(qt, enc, ABT)
            sc, dp = both[:CT] * scale, both[CT:]
            e = jnp.exp(sc - jnp.max(sc, axis=1, keepdims=True))
            p = e / jnp.sum(e, axis=1, keepdims=True)
            dsc = scale * (p * (dp - jnp.sum(dp * p, axis=1, keepdims=True)))
            dsp = jnp.concatenate([dsc.astype(bf), p.astype(bf)], axis=0)
            out = dot(dsp, enc, AB).astype(bf)
            gq_ref[toks, cols] = out[:CT]
            att_ref[toks, cols] = out[CT:]
            denc[rows, cols] = dot(dsp, qt, ATB).astype(bf)
        send(denc, denc_in, d_send, d_recv, g).start()
        store(0, g).start()
        store(1, g).start()
        return 0

    def back(g, _):
        rows = pl.ds(al(g * ROWS, ROWS), ROWS)
        toks = pl.ds(al(g * CT, CT), CT)
        near = dot(denc[rows, :], wo_ref[own, :], AB)
        send(denc, denc_in, d_send, d_recv, g).wait()
        dmix[...] = (near + dot(denc_in[rows, :], wo_ref[other, :], AB)).astype(bf)
        for h in range(heads):
            cols = slice(h * DH, (h + 1) * DH)
            p = probs[g * heads + h]
            dm = dmix[:, cols]
            gv_ref[toks, cols] = dot(p.astype(bf), dm, AB).astype(bf)
            dpe = dot(v_ref[toks, cols], dm, ABT)
            dse = (p * (dpe - jnp.sum(dpe * p, axis=0, keepdims=True))).astype(bf)
            gk_ref[toks, cols] = (scale * dot(dse, encq[rows, cols], AB)).astype(bf)
        store(2, g).start()
        store(3, g).start()
        return 0

    def both(g, _):
        encode(g, 0)
        return cross(g - 2, 0)

    encode(0, 0)
    encode(1, 0)
    weights_on(1)
    w2_on()
    weights_here(1)
    w2_here()
    v_out.wait_recv()
    arrived(48, 64)
    lax.fori_loop(2, SPANS, both, 0)
    lax.fori_loop(SPANS - 2, SPANS, cross, 0)
    for cp in to_pair + rq_copies + list(plus.values()) + list(minus.values()) + list(shares.values()):
        cp.wait_send()
    for n, cp in fcopies.items():
        if n % 16 != 14:
            cp.wait_send()
    for cp in list(wy.values()) + list(ws.values()) + [v_out]:
        cp.wait_send()
    w2_sent()
    lax.fori_loop(0, SPANS, back, 0)
    for n in range(4):
        for g in range(SPANS):
            store(n, g).wait()


def hand_over(*refs):
    inward = [pltpu.make_async_copy(refs[i], refs[8].at[i], refs[9].at[i]) for i in range(4)]
    outward = [pltpu.make_async_copy(refs[8].at[i], refs[4 + i], refs[10].at[i]) for i in range(4)]
    for cp in inward:
        cp.start()
    for i in range(4):
        inward[i].wait()
        outward[i].start()
    for cp in outward:
        cp.wait()


def local(queries, ctx_keys, ctx_values, cotangent, owner, slot_row, database, enc_gain, enc_query_w, enc_out_w):
    dma = pltpu.SemaphoreType.DMA
    bf, f32, i32 = jnp.bfloat16, jnp.float32, jnp.int32
    tokens, half = queries.shape
    full = 2 * half
    rows = SPANS * ROWS
    heads = half // DH
    out = jax.ShapeDtypeStruct((tokens, half), bf)
    vmem, hbm = (pl.BlockSpec(memory_space=sp) for sp in (pltpu.VMEM, pltpu.HBM))
    results = pl.pallas_call(
        kernel,
        out_shape=(out,) * 4,
        in_specs=[hbm, hbm, hbm, vmem] + [hbm] * 6,
        out_specs=(hbm,) * 4,
        scratch_shapes=[
            pltpu.VMEM((tokens, half), bf),
            pltpu.VMEM((tokens, half), bf),
            pltpu.VMEM((tokens, half), bf),
            pltpu.VMEM((tokens, half), bf),
            pltpu.SMEM((K, SPANS), i32),
            pltpu.SMEM((K, SPANS), i32),
            pltpu.VMEM((8, 128), i32),
            pltpu.VMEM((8, 8, 128), i32),
            pltpu.SMEM((8, 8, 128), i32),
            pltpu.VMEM((2, COL, TOK, 128), bf),
            pltpu.VMEM((2, COL, TOK, 128), bf),
            pltpu.VMEM((2, COL, TOK, 128), bf),
            pltpu.VMEM((3, 8, SPANS, K * TOK, 128), bf),
            pltpu.VMEM((12, SPANS, ROWS, 128), bf),
            pltpu.VMEM((full, half), bf),
            pltpu.VMEM((full, half), bf),
            pltpu.VMEM((tokens, half), bf),
            pltpu.VMEM((tokens, half), bf),
            pltpu.VMEM((tokens, half), bf),
            pltpu.VMEM((tokens, half), bf),
            pltpu.VMEM((ROWS, full), bf),
            pltpu.VMEM((rows, half), bf),
            pltpu.VMEM((SPANS * heads, CT, ROWS), f32),
            pltpu.VMEM((SPANS * heads, CT, ROWS), bf),
            pltpu.VMEM((SPANS * heads, CT, ROWS), bf),
            pltpu.VMEM((tokens, half), bf),
            pltpu.VMEM((half, half), bf),
            pltpu.VMEM((ROWS, half), bf),
            pltpu.VMEM((ROWS, half), f32),
            pltpu.VMEM((rows, half), bf),
            pltpu.VMEM((rows, half), bf),
            pltpu.VMEM((ROWS, half), bf),
            dma((12,)), dma((7,)), dma((7,)), dma((24,)), dma((24,)), dma((3,)), dma((3,)),
            dma((21,)), dma((21,)), dma((21,)), dma((21,)), dma((64,)), dma((64,)),
            dma((6,)), dma((6,)), dma((6,)), dma((6,)),
            dma((1,)), dma((1,)), dma((4,)), dma((2,)), dma((2,)), dma((2,)),
            dma((SPANS,)), dma((SPANS,)), dma((SPANS,)), dma((SPANS,)), dma((4, SPANS)),
        ],
        compiler_params=pltpu.CompilerParams(
            collective_id=0, has_side_effects=True, vmem_limit_bytes=63 * 1024 * 1024),
        cost_estimate=pl.CostEstimate(flops=4_600_000_000, bytes_accessed=12_000_000, transcendentals=600_000),
    )(owner.T, slot_row.T, database, enc_gain, enc_query_w, enc_out_w, queries, ctx_keys, ctx_values, cotangent)
    return pl.pallas_call(
        hand_over,
        out_shape=(out,) * 4,
        in_specs=[hbm] * 4,
        out_specs=(hbm,) * 4,
        scratch_shapes=[pltpu.VMEM((4, tokens, half), bf), dma((4,)), dma((4,))],
        cost_estimate=pl.CostEstimate(flops=0, bytes_accessed=4 * tokens * full, transcendentals=0),
    )(*results)


def solution(mesh):
    tokens = P(("section", "shard"), "mp")
    spans = P(("section", "shard"), None)
    weights = P("section", "mp")
    return jax.shard_map(
        local,
        mesh=mesh,
        in_specs=(tokens,) * 4 + (spans, spans, P("shard", None, None), P(), weights, weights),
        out_specs=(tokens,) * 4,
        check_vma=False,
    )
```

```python
import jax
import jax.numpy as jnp
from jax import lax
from jax.experimental import pallas as pl
from jax.experimental.pallas import tpu as pltpu
from jax.sharding import PartitionSpec as P

DH = 128
CT = 64
NT = 64
K = 2
DB = 12
SPANS = 4
REQ = SPANS * K
TOK = NT // 4
COL = 16 * DB
ROWS = K * NT
MESH = pl.DeviceIdType.MESH
AB = ((1,), (0,))
ABT = ((1,), (1,))
ATB = ((0,), (0,))
ORDER = [(ds, dx) for ds in (2, 1, 3, 0) for dx in (1, 0)]
PEERS = [p for p in ORDER if p != (0, 0)]

def dot(a, b, dims):
    return lax.dot_general(a, b, (dims, ((), ())), preferred_element_type=jnp.float32)


def place(t):
    return (t % 3) * 2 + t // 3


def al(v, n):
    return pl.multiple_of(v, n)


def kernel(owner_hbm, row_hbm, db_ref, gain_ref, wq_hbm, wo_hbm, q_hbm, k_hbm, v_hbm, t_hbm,
           att_hbm, gq_hbm, gk_hbm, gv_hbm,
           att_ref, gq_ref, gk_ref, gv_ref, who, row, req, rq, rqs, gath_0, gath_1, gath_2, xm, f_ref, wq_ref, wo_ref, q_ref, k_ref, v_ref, t_ref,
           normed, encq, probs, pb_out, pb_in, v2_ref, w2_ref, mixed, part_own, denc, denc_in, dmix,
           loc, rq_send, rq_recv, sib_send, sib_recv, px_send, px_recv,
           zp_send, zp_recv, zm_send, zm_recv, f_send, f_recv,
           wy_send, wy_recv, ws_send, ws_recv, v_send, v_recv, w2_send, w2_recv, w2s_send, w2s_recv, p_send, p_recv, d_send, d_recv, out_sem):
    s = lax.axis_index("section")
    d = lax.axis_index("shard")
    m = lax.axis_index("mp")
    x, z, c = d // 16, (d // 2) % 8, d % 2
    f32, bf = jnp.float32, jnp.bfloat16
    gath = (gath_0, gath_1, gath_2)

    def dev(s_, x_, z_, c_, m_):
        return (s_, x_ * 16 + z_ * 2 + c_, m_)

    def peer(ds, dx, dm=0):
        return dev((s + ds) % 4, (x + dx) % 2, z, c, (m + dm) % 2)

    pair = peer(0, 1)
    up, down = dev(s, x, (z + 1) % 8, c, m), dev(s, x, (z + 7) % 8, c, m)
    mate = dev(s, x, z, c, 1 - m)
    sib = dev(s, x, z, 1 - c, m)
    me = s * 2 + x

    def remote(src, dst, ss, rs, to):
        return pltpu.make_async_remote_copy(src, dst, ss, rs, device_id=to, device_id_type=MESH)

    friends = [peer(*p) for p in PEERS] + [peer(*p, 1) for p in ORDER] + [sib, up, down]
    barrier = pltpu.get_barrier_semaphore()
    for f in friends:
        pl.semaphore_signal(barrier, inc=1, device_id=f, device_id_type=MESH)

    tok = pl.ds(al(s * TOK, TOK), TOK)

    def feat(column, ch):
        return pl.ds(al(((2 * m + column) * 3 + ch) * 128, 128), 128)

    def blocks(zz):
        return pl.ds(zz * 24 + c * DB, DB)

    small = [pltpu.make_async_copy(owner_hbm, who, loc.at[9]), pltpu.make_async_copy(row_hbm, row, loc.at[10])]
    for cp in small:
        cp.start()
    mine, to_pair = [], []
    for ch in range(3):
        cp = pltpu.make_async_copy(db_ref.at[:, tok, feat(x, ch)], gath[ch].at[x, blocks(z)], loc.at[ch])
        cp.start()
        mine.append(cp)
    pl.semaphore_wait(barrier, len(friends))
    for ch in range(3):
        cp = remote(db_ref.at[:, tok, feat(1 - x, ch)], gath[ch].at[x, blocks(z)], px_send.at[ch], px_recv.at[ch], pair)
        cp.start()
        to_pair.append(cp)
    lane = lax.broadcasted_iota(jnp.int32, (8, 128), 1)
    wanted = jnp.zeros((8, 128), jnp.int32)
    for cp in small:
        cp.wait()
    for j in range(REQ):
        g = who[j % K, j // K] * DB + row[j % K, j // K]
        wanted = jnp.where(lane == j, g, wanted)
    req[...] = wanted
    rq[me] = wanted
    rq_copies = []
    for i, p in enumerate(PEERS):
        cp = remote(req, rq.at[me], rq_send.at[i], rq_recv.at[i], peer(*p))
        cp.start()
        rq_copies.append(cp)

    plus, minus, shares = {}, {}, {}

    def zcopy(ch, k, h, up_way):
        zz = (z + 8 - k) % 8 if up_way else (z + k) % 8
        sl = gath[ch].at[(x + h) % 2, blocks(zz)]
        i = ch * 7 + k * 2 + (h if k < 3 else 0)
        if up_way:
            return remote(sl, sl, zp_send.at[i], zp_recv.at[i], up)
        return remote(sl, sl, zm_send.at[i], zm_recv.at[i], down)

    def share(ch, n, zz):
        sl = gath[ch].at[:, blocks(zz)]
        shares[ch, n] = remote(sl, sl, sib_send.at[ch * 8 + n], sib_recv.at[ch * 8 + n], sib)
        shares[ch, n].start()

    def zstep(ch, k, h):
        if k:
            plus[ch, k - 1, h].wait_recv()
            minus[ch, k - 1, h].wait_recv()
        elif h == 0:
            mine[ch].wait()
        else:
            to_pair[ch].wait_recv()
        for way in (True, False):
            if k < 3 or way == (h == 0):
                cp = zcopy(ch, k, h, way)
                cp.start()
                (plus if way else minus)[ch, k, h] = cp
        if h and k:
            share(ch, 2 * k - 1, (z + 8 - k) % 8)
            share(ch, 2 * k, (z + k) % 8)
        elif h:
            share(ch, 0, z)

    def zdone(ch):
        plus[ch, 3, 0].wait_recv()
        minus[ch, 3, 1].wait_recv()
        share(ch, 7, (z + 4) % 8)
        for n in range(8):
            shares[ch, n].wait_recv()

    loads, wy, ws = {}, {}, {}
    wsrc, wdst = (wq_hbm, wo_hbm), (wq_ref, wo_ref)

    def spans_in():
        for i, (src, dst) in enumerate(((q_hbm, q_ref), (k_hbm, k_ref), (v_hbm, v_ref), (t_hbm, t_ref))):
            loads["qkvt"[i]] = pltpu.make_async_copy(src, dst, loc.at[5 + i])
            loads["qkvt"[i]].start()

    def wcopy(w, ds, sec, to):
        part = wdst[w].at[pl.ds(al(sec * 384 + c * 192, 192), 192)]
        src = wsrc[w].at[pl.ds(al(c * 192, 192), 192)] if ds != 2 else part
        i = w * 3 + ds - 1
        return remote(src, part, wy_send.at[i], wy_recv.at[i], peer(to, 0))

    def weights_out(w):
        loads[w] = pltpu.make_async_copy(wsrc[w], wdst[w].at[pl.ds(al(s * 384, 384), 384)], loc.at[3 + w])
        loads[w].start()
        for ds in (1, 3):
            wy[w, ds] = wcopy(w, ds, s, ds)
            wy[w, ds].start()

    def weights_relay(w):
        ds = (1, 3)[w]
        wy[w, ds].wait_recv()
        wy[w, 2] = wcopy(w, 2, (s + 4 - ds) % 4, ds)
        wy[w, 2].start()

    def weights_on(w):
        for ds in (1, 3, 2):
            if (w, ds) not in ((0, 1), (1, 3)):
                wy[w, ds].wait_recv()
            part = wdst[w].at[pl.ds(al(((s + 4 - ds) % 4) * 384 + c * 192, 192), 192)]
            i = w * 3 + ds - 1
            ws[w, ds] = remote(part, part, ws_send.at[i], ws_recv.at[i], sib)
            ws[w, ds].start()

    def weights_here(w):
        loads[w].wait()
        for ds in (1, 3, 2):
            ws[w, ds].wait_recv()

    v_out = remote(v_hbm, v2_ref, v_send.at[0], v_recv.at[0], mate)

    def w2_rows(u):
        return w2_ref.at[pl.ds(al(u * 384 + c * 192, 192), 192)]

    role = (s + 4 - 2 * m) % 4
    first = ((role + 1) // 2) % 2

    def w2_first():
        return remote(wo_hbm.at[pl.ds(al(c * 192, 192), 192)], w2_rows(s % 2), w2_send.at[0], w2_recv.at[s % 2], mate)

    def w2_next(ds):
        return remote(w2_rows(first), w2_rows(first), w2_send.at[ds], w2_recv.at[first], peer(ds, 0))

    def w2_wait(u):
        remote(w2_rows(u), w2_rows(u), w2_send.at[0], w2_recv.at[u], mate).wait_recv()

    def w2_sib(u):
        return remote(w2_rows(u), w2_rows(u), w2s_send.at[u], w2s_recv.at[u], sib)

    def others_out():
        @pl.when(s // 2 == 1 - m)
        def _():
            w2_first().start()

    def w2_spread():
        @pl.when(role < 2)
        def _():
            w2_wait(first)
            w2_next(1).start()
            w2_next(3).start()

    def w2_relay():
        @pl.when(role == 2)
        def _():
            w2_wait(first)
            w2_next(1).start()

        @pl.when(role == 3)
        def _():
            w2_wait(first)
            w2_next(3).start()

    def w2_on():
        w2_sib(first).start()
        w2_wait(1 - first)
        w2_sib(1 - first).start()

    def w2_here():
        for u in range(2):
            w2_sib(u).wait_recv()

    def w2_sent():
        @pl.when(s // 2 == 1 - m)
        def _():
            w2_first().wait_send()

        @pl.when(role != 3)
        def _():
            w2_next(1).wait_send()

        @pl.when(role != 2)
        def _():
            w2_next(3).wait_send()

        for u in range(2):
            w2_sib(u).wait_send()

    def requests_in():
        for cp in rq_copies:
            cp.wait_recv()
        cp = pltpu.make_async_copy(rq, rqs, loc.at[11])
        cp.start()
        cp.wait()

    fcopies = {}

    def deliver(ch, spans=(0, SPANS), base=None):
        base = ch * 16 if base is None else base
        some = pl.ds(spans[0], spans[1] - spans[0])
        for i, (ds, dx) in enumerate(ORDER):
            for j in range(spans[0] * K, spans[1] * K):
                g = rqs[((s + ds) % 4) * 2 + (x + dx) % 2, 0, j]
                xm[ch, i, j // K, (j % K) * TOK:(j % K + 1) * TOK] = gath[ch][g // COL, lax.rem(g, COL)]
            src = xm.at[ch, i, some]
            dst = f_ref.at[m * 6 + ch * 2 + x, some, pl.ds(al(s * 32, 32), 32), :]
            for dm in (1, 0):
                n = base + i * 2 + dm
                if (ds, dx, dm) == (0, 0, 0):
                    cp = pltpu.make_async_copy(src, dst, f_recv.at[n])
                else:
                    cp = remote(src, dst, f_send.at[n], f_recv.at[n], peer(ds, dx, dm))
                cp.start()
                fcopies[n] = cp

    def arrived(first, last):
        for n in range(first, last):
            if n % 16 == 14:
                fcopies[n].wait()
            else:
                fcopies[n].wait_recv()

    for ch in (0, 2, 1):
        zstep(ch, 0, 0)
    weights_out(0)
    others_out()
    weights_out(1)
    zstep(0, 0, 1)
    zstep(0, 1, 0)
    zstep(1, 1, 0)
    zstep(0, 1, 1)
    zstep(0, 2, 0)
    zstep(1, 0, 1)
    zstep(0, 2, 1)
    zstep(2, 0, 1)
    zstep(1, 1, 1)
    requests_in()
    spans_in()
    weights_relay(0)
    w2_spread()
    v_out.start()
    zstep(0, 3, 0)
    zstep(0, 3, 1)
    zstep(1, 2, 0)
    zstep(1, 2, 1)
    weights_relay(1)
    zstep(2, 1, 0)
    zstep(2, 1, 1)
    zdone(0)
    deliver(0)
    zstep(1, 3, 0)
    zstep(1, 3, 1)
    zstep(2, 2, 0)
    zstep(2, 2, 1)
    zdone(1)
    deliver(1)
    zstep(2, 3, 0)
    zstep(2, 3, 1)
    zdone(2)
    deliver(2, (0, 2), 32)
    deliver(2, (2, 4), 48)
    w2_relay()
    weights_on(0)
    arrived(0, 48)
    weights_here(0)
    for name in "qkvt":
        loads[name].wait()

    scale = DH ** (-0.5)
    heads = q_ref.shape[1] // DH
    width = heads * DH
    own = pl.ds(al(m * width, 128), width)
    other = pl.ds(al((1 - m) * width, 128), width)

    def send_d(g, part):
        block = (pl.ds(al(g * ROWS, ROWS), ROWS), slice(part * (width // 2), (part + 1) * (width // 2)))
        return remote(denc.at[block], denc_in.at[block], d_send.at[g, part], d_recv.at[g, part], mate)

    outs = ((att_ref, att_hbm), (gq_ref, gq_hbm), (gk_ref, gk_hbm), (gv_ref, gv_hbm))

    def store(n, g):
        toks = pl.ds(al(g * CT, CT), CT)
        return pltpu.make_async_copy(outs[n][0].at[toks], outs[n][1].at[toks], out_sem.at[n, g])

    def send_p(g):
        part = pl.ds(g * heads, heads)
        return remote(pb_out.at[part], pb_in.at[part], p_send.at[g], p_recv.at[g], mate)

    def encode(g, _):
        rows = pl.ds(al(g * ROWS, ROWS), ROWS)
        toks = pl.ds(al(g * CT, CT), CT)
        squares = jnp.zeros((ROWS, 128), f32)
        for f in range(12):
            tile = f_ref[f, g].astype(f32)
            squares = squares + tile * tile
        mean = jnp.sum(squares, axis=1, keepdims=True) / (2 * width)
        inv = lax.rsqrt(mean + 1e-06)
        for t in range(12):
            f = (t // 6) * 6 + place(t % 6)
            gain = gain_ref[pl.ds(t * 128, 128)].reshape(1, 128)
            normed[:, t * 128:(t + 1) * 128] = (f_ref[f, g].astype(f32) * inv * gain).astype(bf)
        encq[rows, :] = dot(normed[...], wq_ref[...], AB).astype(bf)
        for h in range(heads):
            cols = slice(h * DH, (h + 1) * DH)
            st = dot(k_ref[toks, cols], encq[rows, cols], ABT) * scale
            e = jnp.exp(st - jnp.max(st, axis=0, keepdims=True))
            p = e * (1.0 / jnp.sum(e, axis=0, keepdims=True))
            probs[g * heads + h] = p
            pb_out[g * heads + h] = p.astype(bf)
        send_p(g).start()
        return 0

    def cross(g, _):
        rows = pl.ds(al(g * ROWS, ROWS), ROWS)
        toks = pl.ds(al(g * CT, CT), CT)
        for h in range(heads):
            cols = slice(h * DH, (h + 1) * DH)
            mixed[:, cols] = dot(pb_out[g * heads + h], v_ref[toks, cols], ATB).astype(bf)
        part_own[...] = dot(mixed[...], wo_ref[own, :], ABT)
        send_p(g).wait()
        for h in range(heads):
            cols = slice(h * DH, (h + 1) * DH)
            mixed[:, cols] = dot(pb_in[g * heads + h], v2_ref[toks, cols], ATB).astype(bf)
        part_own[...] += dot(mixed[...], w2_ref[...], ABT)
        for h in range(heads):
            cols = slice(h * DH, (h + 1) * DH)
            raw = f_ref[m * 6 + place(h), g].astype(f32)
            enc = (raw + part_own[:, cols]).astype(bf)
            qt = jnp.concatenate([q_ref[toks, cols], t_ref[toks, cols]], axis=0)
            both = dot(qt, enc, ABT)
            sc, dp = both[:CT] * scale, both[CT:]
            e = jnp.exp(sc - jnp.max(sc, axis=1, keepdims=True))
            p = e * (1.0 / jnp.sum(e, axis=1, keepdims=True))
            dsc = scale * (p * (dp - jnp.sum(dp * p, axis=1, keepdims=True)))
            dsp = jnp.concatenate([dsc.astype(bf), p.astype(bf)], axis=0)
            out = dot(dsp, enc, AB).astype(bf)
            gq_ref[toks, cols] = out[:CT]
            att_ref[toks, cols] = out[CT:]
            denc[rows, cols] = dot(dsp, qt, ATB).astype(bf)
            if h % 3 == 2:
                send_d(g, h // 3).start()
        store(0, g).start()
        store(1, g).start()
        return 0

    def back(g, _):
        rows = pl.ds(al(g * ROWS, ROWS), ROWS)
        toks = pl.ds(al(g * CT, CT), CT)
        near = dot(denc[rows, :], wo_ref[own, :], AB)
        send_d(g, 0).wait()
        send_d(g, 1).wait()
        dmix[...] = (near + dot(denc_in[rows, :], wo_ref[other, :], AB)).astype(bf)
        for h in range(heads):
            cols = slice(h * DH, (h + 1) * DH)
            p = probs[g * heads + h]
            dm = dmix[:, cols]
            gv_ref[toks, cols] = dot(p.astype(bf), dm, AB).astype(bf)
            dpe = dot(v_ref[toks, cols], dm, ABT)
            dse = (p * (dpe - jnp.sum(dpe * p, axis=0, keepdims=True))).astype(bf)
            gk_ref[toks, cols] = (scale * dot(dse, encq[rows, cols], AB)).astype(bf)
        store(2, g).start()
        store(3, g).start()
        return 0

    def both(g, _):
        encode(g, 0)
        return cross(g - 2, 0)

    encode(0, 0)
    encode(1, 0)
    weights_on(1)
    w2_on()
    weights_here(1)
    w2_here()
    v_out.wait_recv()
    arrived(48, 64)
    lax.fori_loop(2, SPANS, both, 0)
    lax.fori_loop(SPANS - 2, SPANS, cross, 0)
    for cp in to_pair + rq_copies + list(plus.values()) + list(minus.values()) + list(shares.values()):
        cp.wait_send()
    for n, cp in fcopies.items():
        if n % 16 != 14:
            cp.wait_send()
    for cp in list(wy.values()) + list(ws.values()) + [v_out]:
        cp.wait_send()
    w2_sent()
    lax.fori_loop(0, SPANS, back, 0)
    for n in range(4):
        for g in range(SPANS):
            store(n, g).wait()


def hand_over(*refs):
    inward = [pltpu.make_async_copy(refs[i], refs[8].at[i], refs[9].at[i]) for i in range(4)]
    outward = [pltpu.make_async_copy(refs[8].at[i], refs[4 + i], refs[10].at[i]) for i in range(4)]
    for cp in inward:
        cp.start()
    for i in range(4):
        inward[i].wait()
        outward[i].start()
    for cp in outward:
        cp.wait()


def local(queries, ctx_keys, ctx_values, cotangent, owner, slot_row, database, enc_gain, enc_query_w, enc_out_w):
    dma = pltpu.SemaphoreType.DMA
    bf, f32, i32 = jnp.bfloat16, jnp.float32, jnp.int32
    tokens, half = queries.shape
    full = 2 * half
    rows = SPANS * ROWS
    heads = half // DH
    out = jax.ShapeDtypeStruct((tokens, half), bf)
    vmem, hbm = (pl.BlockSpec(memory_space=sp) for sp in (pltpu.VMEM, pltpu.HBM))
    results = pl.pallas_call(
        kernel,
        out_shape=(out,) * 4,
        in_specs=[hbm, hbm, hbm, vmem] + [hbm] * 6,
        out_specs=(hbm,) * 4,
        scratch_shapes=[
            pltpu.VMEM((tokens, half), bf),
            pltpu.VMEM((tokens, half), bf),
            pltpu.VMEM((tokens, half), bf),
            pltpu.VMEM((tokens, half), bf),
            pltpu.SMEM((K, SPANS), i32),
            pltpu.SMEM((K, SPANS), i32),
            pltpu.VMEM((8, 128), i32),
            pltpu.VMEM((8, 8, 128), i32),
            pltpu.SMEM((8, 8, 128), i32),
            pltpu.VMEM((2, COL, TOK, 128), bf),
            pltpu.VMEM((2, COL, TOK, 128), bf),
            pltpu.VMEM((2, COL, TOK, 128), bf),
            pltpu.VMEM((3, 8, SPANS, K * TOK, 128), bf),
            pltpu.VMEM((12, SPANS, ROWS, 128), bf),
            pltpu.VMEM((full, half), bf),
            pltpu.VMEM((full, half), bf),
            pltpu.VMEM((tokens, half), bf),
            pltpu.VMEM((tokens, half), bf),
            pltpu.VMEM((tokens, half), bf),
            pltpu.VMEM((tokens, half), bf),
            pltpu.VMEM((ROWS, full), bf),
            pltpu.VMEM((rows, half), bf),
            pltpu.VMEM((SPANS * heads, CT, ROWS), f32),
            pltpu.VMEM((SPANS * heads, CT, ROWS), bf),
            pltpu.VMEM((SPANS * heads, CT, ROWS), bf),
            pltpu.VMEM((tokens, half), bf),
            pltpu.VMEM((half, half), bf),
            pltpu.VMEM((ROWS, half), bf),
            pltpu.VMEM((ROWS, half), f32),
            pltpu.VMEM((rows, half), bf),
            pltpu.VMEM((rows, half), bf),
            pltpu.VMEM((ROWS, half), bf),
            dma((12,)), dma((7,)), dma((7,)), dma((24,)), dma((24,)), dma((3,)), dma((3,)),
            dma((21,)), dma((21,)), dma((21,)), dma((21,)), dma((64,)), dma((64,)),
            dma((6,)), dma((6,)), dma((6,)), dma((6,)),
            dma((1,)), dma((1,)), dma((4,)), dma((2,)), dma((2,)), dma((2,)),
            dma((SPANS,)), dma((SPANS,)), dma((SPANS, 2)), dma((SPANS, 2)), dma((4, SPANS)),
        ],
        compiler_params=pltpu.CompilerParams(
            collective_id=0, has_side_effects=True, vmem_limit_bytes=63 * 1024 * 1024),
        cost_estimate=pl.CostEstimate(flops=4_600_000_000, bytes_accessed=12_000_000, transcendentals=600_000),
    )(owner.T, slot_row.T, database, enc_gain, enc_query_w, enc_out_w, queries, ctx_keys, ctx_values, cotangent)
    return pl.pallas_call(
        hand_over,
        out_shape=(out,) * 4,
        in_specs=[hbm] * 4,
        out_specs=(hbm,) * 4,
        scratch_shapes=[pltpu.VMEM((4, tokens, half), bf), dma((4,)), dma((4,))],
        cost_estimate=pl.CostEstimate(flops=0, bytes_accessed=4 * tokens * full, transcendentals=0),
    )(*results)


def solution(mesh):
    tokens = P(("section", "shard"), "mp")
    spans = P(("section", "shard"), None)
    weights = P("section", "mp")
    return jax.shard_map(
        local,
        mesh=mesh,
        in_specs=(tokens,) * 4 + (spans, spans, P("shard", None, None), P(), weights, weights),
        out_specs=(tokens,) * 4,
        check_vma=False,
    )
```
